256 devices in a mesh: var: 16 (over x_lo, z), tok: 16 (over y, x_hi, core).
Axes of the slice: x: 4 (x_hi: 2, x_lo: 2; x = x_hi * 2 + x_lo), y: 4, z: 8, core: 2. Of those that a mesh axis runs over, the one named last changes fastest.
Arguments:
- patches: bfloat16 [96, 16, 2048], P('var', None, 'tok'), may hold values from -6 to 6
- slot_variable: int32 [96], P('var'), may hold values from -1 to 90, as said below
- embed_weight: bfloat16 [96, 16, 4096], P('var'), may hold values from -1.5 to 1.5
- variable_embed: bfloat16 [91, 4096], replicated, may hold values from -6 to 6
- norm_gain: bfloat16 [4096], replicated, may hold values from 0.099609375 to 1.8984375
- pool_keys: bfloat16 [4096, 16], replicated, may hold values from -150 to 150
- pool_value: bfloat16 [4096, 2048], P('tok', 'var'), may hold values from -0.09375 to 0.09375
- pool_out: bfloat16 [2048, 4096], P('var'), may hold values from -0.875 to 0.875
- block_gain: bfloat16 [4096], replicated, may hold values from 0.099609375 to 1.8984375
- attend_weight: bfloat16 [3, 4096, 2048], P(None, None, 'var'), may hold values from -6 to 6
- out_proj: bfloat16 [2048, 4096], P('var'), may hold values from -1.25 to 1.25
Outputs:
- aggregated: bfloat16 [2048, 4096], P('tok', 'var')
- attended: bfloat16 [2048, 4096], P('tok', 'var')
The draws below stay inside these ranges and needn't reach their ends.
Inputs may be any that keep to these rules, and one draw needn't show every extreme that they name: `slot_variable`: every variable 0 to 90 stands in exactly one slot; the other 5 slots hold -1 and carry no variable.
All inputs are finite; a program needn't handle non-finite values.
Results may differ from the reference program's by a relative error of at most 0.04.
The reference program's roundings to bfloat16 on the way count: a program that leaves them out, or rounds other values in their place, can miss the bound.
Values may be sent and summed in bfloat16 or wider, within the bound.
No kernel may reach another device: no remote copies, remote signals or barrier semaphores. Data moves between devices by JAX's collectives and lax.ppermute only.
A program may use at most 128 MiB of HBM per device.

```python
import math
import jax
import jax.numpy as jnp
from jax import lax

D = 4096
HEADS = 16
HEAD_DIM = 128
VARS = 91
PATCH = 16
TOK_DEV = 128
VSLOTS = 96
TOKENS = 2048
N_TOK = 16


def draw_slot_variable(key, part):
    key = jax.random.fold_in(key, 11)
    shuffled = jax.random.permutation(key, VSLOTS).astype(jnp.int32)
    return jnp.where(shuffled < VARS, shuffled, -1).astype(jnp.int32)


def draw_pool_keys(key, part):
    key = jax.random.fold_in(key, 12)
    base_key = jax.random.fold_in(key, 0)
    base_draw = jnp.clip(0.35 * jax.random.normal(base_key, (D, HEADS), jnp.float32), -2.1, 2.1)
    return jnp.clip(base_draw, -150.0, 150.0).astype(jnp.bfloat16)


def draw_attend_weight(key, part):
    key = jax.random.fold_in(key, 13)
    base_key = jax.random.fold_in(key, 0)
    deviation = 2.0 / math.sqrt(D)
    base_draw = jnp.clip(jax.random.normal(base_key, (3, D, HEADS * HEAD_DIM), jnp.float32), -6.0, 6.0) * deviation
    return jnp.clip(base_draw, -6.0, 6.0).astype(jnp.bfloat16)


def steps_of(key, extent, cuts, least, high):
    loudness, own = 1.0, jax.random.fold_in(key, 6)
    for position, shards_of in cuts:
        heights = jnp.exp(jax.random.uniform(jax.random.fold_in(own, position), (shards_of,), jnp.float32, least / len(cuts), high / len(cuts)))
        loudness = loudness * jnp.repeat(heights, extent[position] // shards_of).reshape([-1 if axis == position else 1 for axis in range(len(extent))])
    return loudness


def normal_values(key, dims, width, bound, cuts=(), kind=jnp.bfloat16):
    entries = width * jax.random.normal(key, dims, jnp.float32)
    if cuts:
        entries = entries * steps_of(key, dims, cuts, -0.22, 0.18)
    return jnp.clip(entries, -bound, bound).astype(kind)


def setup_inputs(seed: int = 0) -> dict:
    key_of = jax.random.split(jax.random.key(seed), 12)
    patches = normal_values(key_of[0], (VSLOTS, PATCH, TOKENS), 1.0, 6.0, ((0, 16), (2, 16)))
    slot_variable = draw_slot_variable(jax.random.fold_in(key_of[11], 71), 0)
    embed_weight = normal_values(key_of[2], (VSLOTS, PATCH, D), PATCH ** -0.5, 1.5, ((0, 16),))
    variable_embed = normal_values(key_of[3], (VARS, D), 1.0, 6.0)
    norm_gain = jnp.clip(1.0 + 0.18 * jax.random.normal(key_of[4], (D,), jnp.float32), 0.099609375, 1.8984375).astype(jnp.bfloat16)
    pool_keys = draw_pool_keys(jax.random.fold_in(key_of[11], 71), 0)
    pool_value = normal_values(key_of[6], (D, HEADS * HEAD_DIM), D ** -0.5, 0.09375, ((0, 16), (1, 16)))
    pool_out = normal_values(key_of[7], (HEADS * HEAD_DIM, D), (2.5 * (HEADS * HEAD_DIM) ** -0.5), 0.875, ((0, 16),))
    block_gain = jnp.clip(1.0 + 0.18 * jax.random.normal(key_of[8], (D,), jnp.float32), 0.099609375, 1.8984375).astype(jnp.bfloat16)
    attend_weight = draw_attend_weight(jax.random.fold_in(key_of[11], 71), 0)
    out_proj = normal_values(key_of[10], (HEADS * HEAD_DIM, D), (4.0 * (HEADS * HEAD_DIM) ** -0.5), 1.25, ((0, 16),))
    return {"patches": patches, "slot_variable": slot_variable, "embed_weight": embed_weight, "variable_embed": variable_embed, "norm_gain": norm_gain, "pool_keys": pool_keys, "pool_value": pool_value, "pool_out": pool_out, "block_gain": block_gain, "attend_weight": attend_weight, "out_proj": out_proj}


def layer_norm(inputs, gain_vector):
    centered = inputs - lax.optimization_barrier(jnp.mean(inputs, axis=-1, keepdims=True))
    spread = lax.optimization_barrier(jnp.mean(centered * centered, axis=-1, keepdims=True))
    return centered * lax.rsqrt(spread + 1e-05) * gain_vector.astype(jnp.float32)

def reference(patches, slot_variable, embed_weight, variable_embed, norm_gain, pool_keys, pool_value, pool_out, block_gain, attend_weight, out_proj):
    score_scale = 1.0 / math.sqrt(HEAD_DIM)
    occupied = (slot_variable >= 0)[None, :, None]
    lookup = (slot_variable[:, None] == jnp.arange(VARS, dtype=jnp.int32)[None, :]).astype(jnp.bfloat16)
    var_rows = jnp.dot(lookup, variable_embed, preferred_element_type=jnp.float32)
    weight_full = embed_weight.astype(jnp.float32)
    blocks = jnp.transpose(patches.reshape(VSLOTS, PATCH, N_TOK, TOK_DEV), (2, 0, 1, 3))

    def aggregate(patch_block):
        embedded = jnp.einsum('spt,spd->tsd', patch_block.astype(jnp.float32), weight_full, precision=lax.Precision.HIGHEST) + var_rows[None]
        normed = layer_norm(embedded, norm_gain).astype(jnp.bfloat16).reshape(TOK_DEV * VSLOTS, D)
        scores = jnp.dot(normed, pool_keys, preferred_element_type=jnp.float32).reshape(TOK_DEV, VSLOTS, HEADS) * score_scale
        values = jnp.dot(normed, pool_value, preferred_element_type=jnp.float32).reshape(TOK_DEV, VSLOTS, HEADS, HEAD_DIM)
        masked = jnp.where(occupied, scores, -1e+30)
        highest = lax.optimization_barrier(jnp.max(masked, axis=1, keepdims=True))
        weights = jnp.where(occupied, jnp.exp(masked - highest), 0.0)
        numerator = jnp.einsum('tsh,tshe->the', weights, values, precision=lax.Precision.HIGHEST)
        denominator = lax.optimization_barrier(jnp.sum(weights, axis=1))
        pooled = (numerator / denominator[:, :, None]).astype(jnp.bfloat16).reshape(TOK_DEV, HEADS * HEAD_DIM)
        return jnp.dot(pooled, pool_out, preferred_element_type=jnp.float32)
    token_state = lax.map(aggregate, blocks).reshape(TOKENS, D)
    normed_tokens = layer_norm(token_state, block_gain).astype(jnp.bfloat16)
    projected = jnp.einsum('td,cdf->ctf', normed_tokens.astype(jnp.float32), attend_weight.astype(jnp.float32), precision=lax.Precision.HIGHEST).astype(jnp.bfloat16)
    heads_first = jnp.transpose(projected.reshape(3, TOKENS, HEADS, HEAD_DIM), (2, 0, 1, 3))

    def attend(head_stack):
        queries, key_rows, value_rows = (head_stack[0], head_stack[1], head_stack[2])
        scores = jnp.dot(queries, key_rows.T, preferred_element_type=jnp.float32) * score_scale
        row_peak = lax.optimization_barrier(jnp.max(scores, axis=1, keepdims=True))
        unscaled = jnp.exp(scores - row_peak)
        row_total = lax.optimization_barrier(jnp.sum(unscaled, axis=1, keepdims=True))
        return (jnp.dot(unscaled.astype(jnp.bfloat16), value_rows, preferred_element_type=jnp.float32) / row_total).astype(jnp.bfloat16)
    context = lax.map(attend, heads_first)
    context = jnp.transpose(context, (1, 0, 2)).reshape(TOKENS, HEADS * HEAD_DIM)
    attended = jnp.dot(context, out_proj, preferred_element_type=jnp.float32).astype(jnp.bfloat16)
    return (token_state.astype(jnp.bfloat16), attended)
```

```python
import functools
import math

import jax
import jax.numpy as jnp
from jax import lax
from jax.experimental import pallas as pl
from jax.experimental.pallas import tpu as pltpu
from jax.sharding import PartitionSpec as P

F32 = jnp.float32
BF = jnp.bfloat16
N = 16
SLOTS = 6
TOK = 128
COLS = 256
D = 4096
E = 128
SCALE = 1.0 / math.sqrt(128)

R_U0, R_U1, R_P, R_WH, R_WL, R_M, R_ST, R_PC, ROWS = 0, 96, 192, 288, 384, 480, 528, 576, 608


def split2(x):
    hi = x.astype(BF)
    return hi, (x - hi.astype(F32)).astype(BF)


def split3(x):
    hi = x.astype(BF)
    rest = x - hi.astype(F32)
    mid = rest.astype(BF)
    return hi, mid, (rest - mid.astype(F32)).astype(BF)


def call(kernel, out_shape, n_in, scratch=(), smem=(), flops=0, size=0):
    specs = [
        pl.BlockSpec(memory_space=pltpu.SMEM if i in smem else pltpu.VMEM) for i in range(n_in)
    ]
    many = isinstance(out_shape, (tuple, list))
    vm = pl.BlockSpec(memory_space=pltpu.VMEM)
    return pl.pallas_call(
        kernel,
        out_shape=out_shape,
        in_specs=specs,
        out_specs=[vm] * len(out_shape) if many else vm,
        scratch_shapes=list(scratch),
        compiler_params=pltpu.CompilerParams(vmem_limit_bytes=48 * 1024 * 1024),
        cost_estimate=pl.CostEstimate(flops=flops, bytes_accessed=size, transcendentals=0),
    )


def embed_kernel(slot, patches, weight, table, gain, keys, pieces, out, columns, stats):
    wide = table.shape[0]
    row = lax.broadcasted_iota(jnp.int32, (8, wide), 0)
    col = lax.broadcasted_iota(jnp.int32, (8, wide), 1)
    pick = jnp.zeros((8, wide), F32)
    for s in range(SLOTS):
        pick = jnp.where((row == s) & (col == slot[s]), 1.0, pick)
    var_rows = jnp.dot(pick.astype(BF), table[...], preferred_element_type=F32)
    gain_row = gain[...].astype(F32)
    columns[...] = jnp.zeros_like(columns)
    for s in range(SLOTS):
        emb = lax.dot_general(
            patches[s], weight[s], (((0,), (0,)), ((), ())), preferred_element_type=F32
        )
        emb = emb + var_rows[s : s + 1]
        mean = jnp.sum(emb, axis=1, keepdims=True) * (1.0 / D)
        emb = emb - mean
        spread = jnp.sum(emb * emb, axis=1, keepdims=True) * (1.0 / D)
        rstd = lax.rsqrt(spread + 1e-05)
        normed = (emb * rstd * gain_row).astype(BF)
        columns[:, 16 * s : 16 * s + 16] = jnp.dot(
            normed, keys[...], preferred_element_type=F32
        )
        columns[:, 96 + s : 97 + s] = mean
        columns[:, 102 + s : 103 + s] = rstd
    turned = jnp.transpose(columns[...])
    scores = [
        jnp.where(slot[s] >= 0, turned[16 * s : 16 * s + 16] * SCALE, -1e30) for s in range(SLOTS)
    ]
    top = scores[0]
    for s in range(1, SLOTS):
        top = jnp.maximum(top, scores[s])
    w_hi, w_lo = [], []
    for s in range(SLOTS):
        hi, lo = split2(jnp.where(slot[s] >= 0, jnp.exp(scores[s] - top), 0.0))
        w_hi.append(hi)
        w_lo.append(lo)
    tops = split3(top)
    means = split3(turned[96:102])
    rstds = split3(turned[102:108])
    for i in range(3):
        stats[6 * i : 6 * i + 6] = means[i].astype(F32)
        stats[18 + 6 * i : 24 + 6 * i] = rstds[i].astype(F32)
    for v in range(N):
        for s in range(SLOTS):
            a = 16 * s
            out[v, R_U0 + a : R_U0 + a + 16] = weight[s, :, COLS * v : COLS * v + 128]
            out[v, R_U1 + a : R_U1 + a + 16] = weight[s, :, COLS * v + 128 : COLS * v + 256]
            out[v, R_P + a : R_P + a + 16] = patches[s]
            out[v, R_WH + a : R_WH + a + 16] = w_hi[s]
            out[v, R_WL + a : R_WL + a + 16] = w_lo[s]
        for i in range(3):
            out[v, R_M + 16 * i : R_M + 16 * i + 16] = tops[i]
        stats[36:42] = var_rows[:6, COLS * v : COLS * v + 128]
        stats[42:48] = var_rows[:6, COLS * v + 128 : COLS * v + 256]
        out[v, R_ST : R_ST + 48] = stats[...].astype(BF)
        out[v, R_PC : R_PC + 32] = pieces[v]


def pool_kernel(got, gain, value, out, weights, turned, rows, summed):
    tops = []
    for v in range(N):
        m = [got[v, R_M + 16 * i : R_M + 16 * i + 16].astype(F32) for i in range(3)]
        tops.append((m[0] + m[1]) + m[2])
    top = tops[0]
    for v in range(1, N):
        top = jnp.maximum(top, tops[v])
    total = jnp.zeros((16, TOK), F32)
    for v in range(N):
        factor = jnp.exp(tops[v] - top)
        for s in range(SLOTS):
            a = 16 * s
            w = got[v, R_WH + a : R_WH + a + 16].astype(F32) + got[
                v, R_WL + a : R_WL + a + 16
            ].astype(F32)
            w = w * factor
            total = total + w
            weights[96 * v + a : 96 * v + a + 16] = w
    inverse = 1.0 / total
    for h in range(N):
        w = weights[pl.ds(h, 96, stride=16)] * inverse[h : h + 1]
        w = jnp.transpose(jnp.concatenate([w, jnp.zeros((32, TOK), F32)], 0))
        hi = w.astype(BF).astype(F32)
        turned[pl.ds(h, TOK, stride=32)] = hi
        turned[pl.ds(16 + h, TOK, stride=32)] = (w - hi).astype(BF).astype(F32)
    gain_row = gain[...].astype(F32)

    def source(v, carry):
        st = got[v, R_ST : R_ST + 48].astype(F32)
        mean = (st[0:6] + st[6:12]) + st[12:18]
        rstd = (st[18:24] + st[24:30]) + st[30:36]
        both = jnp.concatenate([mean, rstd, jnp.zeros((116, TOK), F32)], 0)
        both = jnp.transpose(both)
        var0, var1 = st[36:42], st[42:48]
        for s in range(SLOTS):
            a = 16 * s
            p = got[v, R_P + a : R_P + a + 16]
            col_mean, col_rstd = both[:, s : s + 1], both[:, 6 + s : 7 + s]
            for half, var in ((0, var0), (1, var1)):
                u = got[v, 96 * half + a : 96 * half + a + 16]
                emb = lax.dot_general(
                    p, u, (((0,), (0,)), ((), ())), preferred_element_type=F32
                )
                emb = emb + var[s : s + 1]
                x = (emb - col_mean) * col_rstd * gain_row[:, 128 * half : 128 * half + 128]
                rows[half, pl.ds(6 * v + s, TOK, stride=96)] = x
        return carry

    lax.fori_loop(0, N, source, 0)

    def token(t, carry):
        at = pl.multiple_of(t * 96, 8)
        lhs = turned[pl.ds(pl.multiple_of(t * 32, 32), 32)].astype(BF)[:, :96]
        for half in range(2):
            rhs = rows[half, pl.ds(at, 96)].astype(BF)
            y = jnp.dot(lhs, rhs, preferred_element_type=F32)
            summed[half, pl.ds(t, 16, stride=TOK)] = y[:16] + y[16:]
        return carry

    lax.fori_loop(0, TOK, token, 0, unroll=8)
    for h in range(N):
        at = pl.ds(TOK * h, TOK)
        hi, lo = split2(jnp.concatenate([summed[0, at], summed[1, at]], 1))
        out[h] = jnp.dot(hi, value[h], preferred_element_type=F32) + jnp.dot(
            lo, value[h], preferred_element_type=F32
        )


def pooled_kernel(got, out):
    total = got[0]
    for v in range(1, N):
        total = total + got[v]
    total = total.astype(BF)
    for v in range(N):
        out[v] = total


def columns_of(blocks, weight):
    halves = []
    for half in range(2):
        acc = None
        for h in range(0, N, 2):
            left = jnp.concatenate([blocks[h], blocks[h + 1]], 1)
            right = jnp.concatenate(
                [weight[2 * j + half, h + i] for i in range(2) for j in range(8)], 0
            )
            term = jnp.dot(left, right, preferred_element_type=F32)
            acc = term if acc is None else acc + term
        halves.append(acc)
    return halves


def state_kernel(got, weight, state, aggregated, stats, columns):
    halves = columns_of(got, weight)
    mean = (
        jnp.sum(halves[0], axis=1, keepdims=True) + jnp.sum(halves[1], axis=1, keepdims=True)
    ) * (1.0 / COLS)
    spread = None
    for i in range(2):
        state[:, 128 * i : 128 * i + 128] = halves[i]
        aggregated[:, 128 * i : 128 * i + 128] = halves[i].astype(BF)
        c = halves[i] - mean
        term = jnp.sum(c * c, axis=1, keepdims=True)
        spread = term if spread is None else spread + term
    columns[...] = jnp.zeros_like(columns)
    columns[:, 0:1] = mean
    columns[:, 1:2] = spread
    turned = jnp.transpose(columns[...])[0:8]
    for v in range(N):
        stats[v] = turned


def norm_kernel(got, state, gain, out):
    mean = got[0, 0:1]
    for v in range(1, N):
        mean = mean + got[v, 0:1]
    mean = mean * (1.0 / N)
    spread = jnp.zeros((1, TOK), F32)
    for v in range(N):
        gap = got[v, 0:1] - mean
        spread = spread + (got[v, 1:2] + COLS * gap * gap)
    rstd = lax.rsqrt(spread * (1.0 / D) + 1e-05)
    both = jnp.transpose(jnp.concatenate([mean, rstd, jnp.zeros((126, TOK), F32)], 0))
    normed = ((state[...] - both[:, 0:1]) * both[:, 1:2] * gain[...].astype(F32)).astype(BF)
    for v in range(N):
        out[v] = normed


def project_kernel(got, weight, query, out):
    for c in range(3):
        acc = None
        for v in range(N):
            term = jnp.dot(
                got[v], weight[c, COLS * v : COLS * v + COLS], preferred_element_type=F32
            )
            acc = term if acc is None else acc + term
        acc = acc.astype(BF)
        if c == 0:
            query[...] = acc
        else:
            for k in range(N):
                out[k, TOK * (c - 1) : TOK * c] = acc


def attend_kernel(query, got, out, scores):
    q = query[...]
    peak = None
    for k in range(N):
        s = (
            lax.dot_general(
                q, got[k, 0:TOK], (((1,), (1,)), ((), ())), preferred_element_type=F32
            )
            * SCALE
        )
        scores[:, TOK * k : TOK * k + TOK] = s
        peak = s if peak is None else jnp.maximum(peak, s)
    peak = jnp.max(peak, axis=1, keepdims=True)
    total, acc = None, None
    for k in range(N):
        e = jnp.exp(scores[:, TOK * k : TOK * k + TOK] - peak)
        total = e if total is None else total + e
        term = jnp.dot(e.astype(BF), got[k, TOK : 2 * TOK], preferred_element_type=F32)
        acc = term if acc is None else acc + term
    context = (acc / jnp.sum(total, axis=1, keepdims=True)).astype(BF)
    for v in range(N):
        out[v] = context


def output_kernel(got, weight, out):
    halves = columns_of(got, weight)
    for i in range(2):
        out[:, 128 * i : 128 * i + 128] = halves[i].astype(BF)


def shape(dims, kind):
    return jax.ShapeDtypeStruct(dims, kind)


def exchange(x, axis):
    return lax.all_to_all(x, axis, 0, 0, tiled=True)


def shards(
    patches,
    slot_variable,
    embed_weight,
    variable_embed,
    norm_gain,
    pool_keys,
    pool_value,
    pool_out,
    block_gain,
    attend_weight,
    out_proj,
):
    v_idx, k_idx = lax.axis_index("var"), lax.axis_index("tok")

    swap = [(v * N + k, k * N + v) for v in range(N) for k in range(N)]
    value = lax.ppermute(pool_value, ("var", "tok"), swap)
    value = lax.all_gather(value, "tok", axis=0)

    def piece(weight):
        rows = lax.dynamic_slice(weight, (16 * (k_idx // 2), 0), (16, D))
        rows = rows.reshape(16, N, 2, 128)
        rows = lax.dynamic_index_in_dim(rows, k_idx % 2, 2, keepdims=False)
        return jnp.transpose(rows, (1, 0, 2))

    pieces = jnp.concatenate([piece(pool_out), piece(out_proj)], 1)
    packed = call(
        embed_kernel,
        shape((N, ROWS, 128), BF),
        7,
        (pltpu.VMEM((TOK, 128), F32), pltpu.VMEM((48, 128), F32)),
        smem=(0,),
        flops=2 * SLOTS * TOK * D * 48,
        size=6_000_000,
    )(
        slot_variable,
        patches,
        embed_weight,
        variable_embed,
        norm_gain[None],
        pool_keys,
        pieces,
    )
    got = exchange(packed, "var")
    out_rows = lax.all_gather(got[:, R_PC : R_PC + 16], "tok", axis=0)
    proj_rows = lax.all_gather(got[:, R_PC + 16 : R_PC + 32], "tok", axis=0)

    def own_columns(gain):
        return lax.dynamic_slice(gain, (COLS * v_idx,), (COLS,))[None]

    partial = call(
        pool_kernel,
        shape((N, TOK, E), F32),
        3,
        (
            pltpu.VMEM((96 * N, TOK), F32),
            pltpu.VMEM((TOK * 32, TOK), F32),
            pltpu.VMEM((2, TOK * 96, 128), F32),
            pltpu.VMEM((2, N * TOK, 128), F32),
        ),
        flops=2 * 400_000_000,
        size=5_000_000,
    )(got, own_columns(norm_gain), value)
    pooled = call(pooled_kernel, shape((N, TOK, E), BF), 1, size=1_500_000)(
        exchange(partial, "var")
    )
    state, aggregated, stats = call(
        state_kernel,
        (shape((TOK, COLS), F32), shape((TOK, COLS), BF), shape((N, 8, 128), F32)),
        2,
        (pltpu.VMEM((TOK, 128), F32),),
        flops=2 * TOK * 2048 * COLS,
        size=2_000_000,
    )(exchange(pooled, "var"), out_rows)
    normed = call(norm_kernel, shape((N, TOK, COLS), BF), 3, size=1_200_000)(
        exchange(stats, "var"), state, own_columns(block_gain)
    )
    query, kv = call(
        project_kernel,
        (shape((TOK, E), BF), shape((N, 2 * TOK, E), BF)),
        2,
        flops=2 * TOK * D * 384,
        size=5_000_000,
    )(exchange(normed, "var"), attend_weight)
    context = call(
        attend_kernel,
        shape((N, TOK, E), BF),
        2,
        (pltpu.VMEM((TOK, N * TOK), F32),),
        flops=4 * TOK * 2048 * E,
        size=1_500_000,
    )(query, exchange(kv, "tok"))
    attended = call(
        output_kernel, shape((TOK, COLS), BF), 2, flops=2 * TOK * 2048 * COLS, size=2_000_000
    )(exchange(context, "var"), proj_rows)
    return (aggregated, attended)


def solution(mesh):
    return jax.shard_map(
        shards,
        mesh=mesh,
        in_specs=(
            P("var", None, "tok"),
            P("var"),
            P("var", None, None),
            P(),
            P(),
            P(),
            P("tok", "var"),
            P("var", None),
            P(),
            P(None, None, "var"),
            P("var", None),
        ),
        out_specs=(P("tok", "var"), P("tok", "var")),
        check_vma=False,
    )
```

```python
import functools
import math

import jax
import jax.numpy as jnp
from jax import lax
from jax.experimental import pallas as pl
from jax.experimental.pallas import tpu as pltpu
from jax.sharding import PartitionSpec as P

F32 = jnp.float32
BF = jnp.bfloat16
N = 16
SLOTS = 6
TOK = 128
COLS = 256
D = 4096
E = 128
SCALE = 1.0 / math.sqrt(128)

Z = 8
WIDE = 512
HALF = 48


R_U, R_P, R_WH, R_WL, R_M, R_ST, ROWS = 0, 384, 480, 576, 672, 720, 784
W_V, W_P, W_O, W_ROWS = 0, 32, 48, 64


def split2(x):
    hi = x.astype(BF)
    return hi, (x - hi.astype(F32)).astype(BF)


def split3(x):
    hi = x.astype(BF)
    rest = x - hi.astype(F32)
    mid = rest.astype(BF)
    return hi, mid, (rest - mid.astype(F32)).astype(BF)


def call(
    kernel, out_shape, n_in, scratch=(), smem=(), unread=(), blocks=None, vmem=24, flops=0, size=0
):
    many = isinstance(out_shape, (tuple, list))
    shapes = list(out_shape) if many else [out_shape]
    spaces = {i: pltpu.SMEM for i in smem} | {i: pl.ANY for i in unread}
    blocks = blocks or {}
    specs = []
    for i in range(n_in):
        if i in blocks:
            part, index = blocks[i]
            specs.append(pl.BlockSpec(part, index, pipeline_mode=pl.Buffered(1)))
        else:
            specs.append(pl.BlockSpec(memory_space=spaces.get(i, pltpu.VMEM)))
    outs = [pl.BlockSpec(memory_space=pltpu.VMEM)] * len(shapes)
    return pl.pallas_call(
        kernel,
        out_shape=out_shape,
        grid=(1,) if blocks else (),
        in_specs=specs,
        out_specs=outs if many else outs[0],
        scratch_shapes=list(scratch),
        compiler_params=pltpu.CompilerParams(vmem_limit_bytes=vmem * 1024 * 1024),
        cost_estimate=pl.CostEstimate(flops=flops, bytes_accessed=size, transcendentals=0),
    )


def weights_kernel(place, value, pool_rows, proj_rows, out):
    half = place[0] % 2
    for v in range(N):
        z = v % Z
        out[v, W_V : W_V + 32] = value[32 * z : 32 * z + 32]
        at = pl.ds(pl.multiple_of(COLS * v + 128 * half, 128), 128)
        out[v, W_P : W_P + 16] = pool_rows[:, at]
        out[v, W_O : W_O + 16] = proj_rows[:, at]


def embed_kernel(slot, patches, weight, table, gain, keys, common, var_out, columns):
    wide = table.shape[0]
    row = lax.broadcasted_iota(jnp.int32, (8, wide), 0)
    col = lax.broadcasted_iota(jnp.int32, (8, wide), 1)
    pick = jnp.zeros((8, wide), F32)
    for s in range(SLOTS):
        pick = jnp.where((row == s) & (col == slot[s]), 1.0, pick)
    var_rows = jnp.dot(pick.astype(BF), table[...], preferred_element_type=F32)
    var_out[...] = var_rows
    gain_row = gain[...].astype(F32)
    columns[...] = jnp.zeros_like(columns)
    scores = []
    for s in range(SLOTS):
        emb = lax.dot_general(
            patches[s], weight[s], (((0,), (0,)), ((), ())), preferred_element_type=F32
        )
        emb = emb + var_rows[s : s + 1]
        mean = jnp.sum(emb, axis=1, keepdims=True) * (1.0 / D)
        emb = emb - mean
        spread = jnp.sum(emb * emb, axis=1, keepdims=True) * (1.0 / D)
        rstd = lax.rsqrt(spread + 1e-05)
        normed = (emb * rstd * gain_row).astype(BF)
        score = lax.dot_general(
            keys[...], normed, (((1,), (1,)), ((), ())), preferred_element_type=F32
        )
        scores.append(jnp.where(slot[s] >= 0, score * SCALE, -1e30))
        columns[:, s : s + 1] = mean
        columns[:, 6 + s : 7 + s] = rstd
    turned = jnp.transpose(columns[...])
    top = scores[0]
    for s in range(1, SLOTS):
        top = jnp.maximum(top, scores[s])
    for s in range(SLOTS):
        a = 16 * s
        hi, lo = split2(jnp.where(slot[s] >= 0, jnp.exp(scores[s] - top), 0.0))
        common[R_P - R_P + a : R_P - R_P + a + 16] = patches[s]
        common[R_WH - R_P + a : R_WH - R_P + a + 16] = hi
        common[R_WL - R_P + a : R_WL - R_P + a + 16] = lo
    tops = split3(top)
    stats = []
    for rows in (turned[0:6], turned[6:12]):
        stats.extend(x.astype(F32) for x in split3(rows))
    stats.append(jnp.zeros((28, TOK), F32))
    for i in range(3):
        common[R_M - R_P + 16 * i : R_M - R_P + 16 * i + 16] = tops[i]
    common[R_ST - R_P :] = jnp.concatenate(stats, 0).astype(BF)


def chunks(x, z, j):
    at = [256 * k + 32 * z for k in range(4 * j, 4 * j + 4)]
    return jnp.concatenate([x[:, a : a + 32] for a in at], 1)


def pack_kernel(weight, common, var_rows, early, out):
    for s in range(SLOTS):
        wide = weight[s].astype(F32)
        for z in range(Z):
            for j in range(4):
                a = R_U + 96 * j + 16 * s
                out[z, a : a + 16] = chunks(wide, z, j).astype(BF)
    stats = common[R_ST - R_P :].astype(F32)[:36]
    for z in range(Z):
        out[z, R_P:R_ST] = common[0 : R_ST - R_P]
        rows = [stats] + [chunks(var_rows[...], z, j)[:6] for j in range(4)]
        rows.append(jnp.zeros((4, TOK), F32))
        out[z, R_ST:] = jnp.concatenate(rows, 0).astype(BF)


def pool_kernel(got, gain, summed, tails, weights, turned, rows):
    tops = []
    for z in range(Z):
        m = [got[z, R_M + 16 * i : R_M + 16 * i + 16].astype(F32) for i in range(3)]
        tops.append((m[0] + m[1]) + m[2])
    top = tops[0]
    for z in range(1, Z):
        top = jnp.maximum(top, tops[z])
    total = jnp.zeros((16, TOK), F32)
    for z in range(Z):
        factor = jnp.exp(tops[z] - top)
        for s in range(SLOTS):
            a = 16 * s
            w = got[z, R_WH + a : R_WH + a + 16].astype(F32) + got[
                z, R_WL + a : R_WL + a + 16
            ].astype(F32)
            w = w * factor
            total = total + w
            weights[96 * z + a : 96 * z + a + 16] = w
    lane = lax.broadcasted_iota(jnp.int32, (HALF, TOK), 1)
    for h in range(N):
        w = weights[pl.ds(h, HALF, stride=16)]
        parts = [jnp.where(lane % 4 == q, w, 0.0) for q in range(4)]
        parts.append(jnp.zeros((256 - 4 * HALF, TOK), F32))
        w = jnp.concatenate(parts, 0)
        for i in range(2):
            part = jnp.transpose(w[128 * i : 128 * i + 128])
            hi = part.astype(BF).astype(F32)
            turned[i, pl.ds(h, TOK, stride=32)] = hi
            turned[i, pl.ds(16 + h, TOK, stride=32)] = (part - hi).astype(BF).astype(F32)
    gain_row = gain[...].astype(F32)

    def source(z, carry):
        st = got[z, R_ST : R_ST + 64].astype(F32)
        mean = (st[0:6] + st[6:12]) + st[12:18]
        rstd = (st[18:24] + st[24:30]) + st[30:36]
        both = jnp.transpose(jnp.concatenate([mean, rstd, jnp.zeros((116, TOK), F32)], 0))
        for s in range(SLOTS):
            a = 16 * s
            p = got[z, R_P + a : R_P + a + 16]
            col_mean, col_rstd = both[:, s : s + 1], both[:, 6 + s : 7 + s]
            for i in range(2):
                u = jnp.concatenate(
                    [got[z, 96 * j + a : 96 * j + a + 16] for j in (2 * i, 2 * i + 1)], 1
                )
                emb = lax.dot_general(
                    p, u, (((0,), (0,)), ((), ())), preferred_element_type=F32
                )
                for n in range(2):
                    j = 2 * i + n
                    var = st[36 + 6 * j + s : 37 + 6 * j + s]
                    x = emb[:, 128 * n : 128 * n + 128] + var
                    x = (x - col_mean) * col_rstd * gain_row[:, 128 * j : 128 * j + 128]
                    rows[j, pl.ds(6 * z + s, TOK, stride=HALF)] = x
        return carry

    lax.fori_loop(0, Z, source, 0)

    def four_tokens(g, carry):
        at = pl.ds(pl.multiple_of(g * 128, 128), 128)
        lhs = jnp.concatenate([turned[0, at], turned[1, at][:, : 4 * HALF - 128]], 1).astype(BF)
        span = pl.ds(pl.multiple_of(g * 4 * HALF, 4 * HALF), 4 * HALF)
        for i in range(2):
            rhs = jnp.concatenate([rows[2 * i, span], rows[2 * i + 1, span]], 1).astype(BF)
            y = jnp.dot(lhs, rhs, preferred_element_type=F32)
            for q in range(4):
                part = y[32 * q : 32 * q + 16] + y[32 * q + 16 : 32 * q + 32]
                for n in range(2):
                    summed[2 * i + n, pl.ds(4 * g + q, 16, stride=TOK)] = part[
                        :, 128 * n : 128 * n + 128
                    ]
        return carry

    lax.fori_loop(0, TOK // 4, four_tokens, 0, unroll=4)
    tails[0] = top
    tails[1] = total


def values_kernel(summed, tails, value, out):
    for h in range(N):
        at = pl.ds(TOK * h, TOK)
        hi, lo = split2(jnp.concatenate([summed[j, at] for j in range(4)], 1))
        right = jnp.concatenate([value[k, h] for k in range(N)], 0)
        out[h, 0:TOK] = jnp.dot(hi, right, preferred_element_type=F32) + jnp.dot(
            lo, right, preferred_element_type=F32
        )
        out[h, TOK : TOK + 1] = tails[0, h : h + 1]
        out[h, TOK + 1 : TOK + 2] = tails[1, h : h + 1]
        out[h, TOK + 2 : TOK + 8] = jnp.zeros((6, TOK), F32)


def pooled_kernel(got, out):
    tops = [got[Z * x, TOK : TOK + 1] for x in range(2)]
    totals = [got[Z * x, TOK + 1 : TOK + 2] for x in range(2)]
    top = jnp.maximum(tops[0], tops[1])
    factors = [jnp.exp(t - top) for t in tops]
    total = factors[0] * totals[0] + factors[1] * totals[1]
    both = jnp.concatenate([f / total for f in factors] + [jnp.zeros((126, TOK), F32)], 0)
    both = jnp.transpose(both)
    pooled = None
    for x in range(2):
        part = got[Z * x, 0:TOK]
        for z in range(1, Z):
            part = part + got[Z * x + z, 0:TOK]
        part = part * both[:, x : x + 1]
        pooled = part if pooled is None else pooled + part
    pooled = pooled.astype(BF)
    for v in range(N):
        out[v] = pooled


def columns_of(blocks, weight):
    halves = []
    for half in range(2):
        acc = None
        for h in range(0, N, 2):
            left = jnp.concatenate([blocks[h], blocks[h + 1]], 1)
            right = jnp.concatenate(
                [weight[2 * j + half, h + i] for i in range(2) for j in range(8)], 0
            )
            term = jnp.dot(left, right, preferred_element_type=F32)
            acc = term if acc is None else acc + term
        halves.append(acc)
    return halves


def state_kernel(got, weight, state, aggregated, stats, columns):
    halves = columns_of(got, weight)
    mean = (
        jnp.sum(halves[0], axis=1, keepdims=True) + jnp.sum(halves[1], axis=1, keepdims=True)
    ) * (1.0 / COLS)
    spread = None
    for i in range(2):
        state[:, 128 * i : 128 * i + 128] = halves[i]
        aggregated[:, 128 * i : 128 * i + 128] = halves[i].astype(BF)
        c = halves[i] - mean
        term = jnp.sum(c * c, axis=1, keepdims=True)
        spread = term if spread is None else spread + term
    columns[...] = jnp.zeros_like(columns)
    columns[:, 0:1] = mean
    columns[:, 1:2] = spread
    turned = jnp.transpose(columns[...])[0:8]
    for v in range(N):
        stats[v] = turned


def norm_kernel(got, state, gain, out):
    mean = got[0, 0:1]
    for v in range(1, N):
        mean = mean + got[v, 0:1]
    mean = mean * (1.0 / N)
    spread = jnp.zeros((1, TOK), F32)
    for v in range(N):
        gap = got[v, 0:1] - mean
        spread = spread + (got[v, 1:2] + COLS * gap * gap)
    rstd = lax.rsqrt(spread * (1.0 / D) + 1e-05)
    both = jnp.transpose(jnp.concatenate([mean, rstd, jnp.zeros((126, TOK), F32)], 0))
    normed = ((state[...] - both[:, 0:1]) * both[:, 1:2] * gain[...].astype(F32)).astype(BF)
    for v in range(N):
        out[v] = normed


def project_kernel(got, weight, query, out):
    for c in range(3):
        acc = None
        for v in range(N):
            term = jnp.dot(
                got[v], weight[c, COLS * v : COLS * v + COLS], preferred_element_type=F32
            )
            acc = term if acc is None else acc + term
        acc = acc.astype(BF)
        if c == 0:
            query[...] = acc
        else:
            for k in range(N):
                out[k, TOK * (c - 1) : TOK * c] = acc


def attend_kernel(query, got, out, scores):
    q = query[...]
    peak = None
    for k in range(N):
        s = (
            lax.dot_general(
                q, got[k, 0:TOK], (((1,), (1,)), ((), ())), preferred_element_type=F32
            )
            * SCALE
        )
        scores[:, TOK * k : TOK * k + TOK] = s
        peak = s if peak is None else jnp.maximum(peak, s)
    peak = jnp.max(peak, axis=1, keepdims=True)
    total, acc = None, None
    for k in range(N):
        e = jnp.exp(scores[:, TOK * k : TOK * k + TOK] - peak)
        total = e if total is None else total + e
        term = jnp.dot(e.astype(BF), got[k, TOK : 2 * TOK], preferred_element_type=F32)
        acc = term if acc is None else acc + term
    context = (acc / jnp.sum(total, axis=1, keepdims=True)).astype(BF)
    for v in range(N):
        out[v] = context


def output_kernel(got, weight, out):
    halves = columns_of(got, weight)
    for i in range(2):
        out[:, 128 * i : 128 * i + 128] = halves[i].astype(BF)


def shape(dims, kind):
    return jax.ShapeDtypeStruct(dims, kind)


def exchange(x, axis):
    return lax.all_to_all(x, axis, 0, 0, tiled=True)


def shards(
    patches,
    slot_variable,
    embed_weight,
    variable_embed,
    norm_gain,
    pool_keys,
    pool_value,
    pool_out,
    block_gain,
    attend_weight,
    out_proj,
):
    v_idx, k_idx = lax.axis_index("var"), lax.axis_index("tok")
    place = jnp.stack([k_idx, k_idx // 2]).astype(jnp.int32)

    rows_of_k = pl.BlockSpec((16, D), lambda i, place: (place[1], 0))
    parts = pl.pallas_call(
        weights_kernel,
        out_shape=shape((N, W_ROWS, 128), BF),
        grid_spec=pltpu.PrefetchScalarGridSpec(
            num_scalar_prefetch=1,
            grid=(1,),
            in_specs=[pl.BlockSpec((COLS, E), lambda i, place: (0, 0)), rows_of_k, rows_of_k],
            out_specs=pl.BlockSpec((N, W_ROWS, 128), lambda i, place: (0, 0, 0)),
        ),
        cost_estimate=pl.CostEstimate(flops=0, bytes_accessed=800_000, transcendentals=0),
    )(place, pool_value, pool_out, out_proj)
    parts = exchange(parts, "var")
    common, var_rows = call(
        embed_kernel,
        (shape((ROWS - R_P, TOK), BF), shape((8, D), F32)),
        6,
        (pltpu.VMEM((TOK, 128), F32),),
        smem=(0,),
        flops=2 * SLOTS * TOK * D * 48,
        size=4_000_000,
    )(
        slot_variable,
        patches,
        embed_weight,
        variable_embed,
        norm_gain[None],
        pool_keys.T,
    )
    packed = call(pack_kernel, shape((Z, ROWS, 128), BF), 4, unread=(3,), size=3_000_000)(
        embed_weight, common, var_rows, parts
    )
    parts = lax.all_gather(parts, "tok", axis=0)
    rings = [list(range(Z)), list(range(Z, N))]
    got = lax.all_to_all(packed, "var", 0, 0, tiled=True, axis_index_groups=rings)
    gain = lax.dynamic_index_in_dim(norm_gain.reshape(N, Z, 32), v_idx % Z, 1, keepdims=False)

    summed, tails = call(
        pool_kernel,
        (shape((4, N * TOK, 128), F32), shape((2, N, TOK), F32)),
        2,
        (
            pltpu.VMEM((96 * Z, TOK), F32),
            pltpu.VMEM((2, TOK * 32, TOK), F32),
            pltpu.VMEM((4, TOK * HALF, 128), F32),
        ),
        vmem=36,
        flops=2 * 400_000_000,
        size=5_000_000,
    )(got, gain.reshape(1, WIDE))
    partial = call(
        values_kernel,
        shape((N, TOK + 8, E), F32),
        3,
        blocks={2: ((N, N, 32, E), lambda i: (0, 0, 0, 0))},
        flops=4 * TOK * WIDE * 2048,
        size=7_000_000,
    )(summed, tails, parts)
    pooled = call(pooled_kernel, shape((N, TOK, E), BF), 1, size=1_500_000)(
        exchange(partial, "var")
    )
    state, aggregated, stats = call(
        state_kernel,
        (shape((TOK, COLS), F32), shape((TOK, COLS), BF), shape((N, 8, 128), F32)),
        2,
        (pltpu.VMEM((TOK, 128), F32),),
        blocks={1: ((N, N, 16, 128), lambda i: (0, 0, W_P // 16, 0))},
        flops=2 * TOK * 2048 * COLS,
        size=2_000_000,
    )(exchange(pooled, "var"), parts)
    normed = call(norm_kernel, shape((N, TOK, COLS), BF), 3, size=1_200_000)(
        exchange(stats, "var"),
        state,
        lax.dynamic_slice(block_gain, (COLS * v_idx,), (COLS,))[None],
    )
    query, kv = call(
        project_kernel,
        (shape((TOK, E), BF), shape((N, 2 * TOK, E), BF)),
        2,
        flops=2 * TOK * D * 384,
        size=5_000_000,
    )(exchange(normed, "var"), attend_weight)
    context = call(
        attend_kernel,
        shape((N, TOK, E), BF),
        2,
        (pltpu.VMEM((TOK, N * TOK), F32),),
        flops=4 * TOK * 2048 * E,
        size=1_500_000,
    )(query, exchange(kv, "tok"))
    attended = call(
        output_kernel,
        shape((TOK, COLS), BF),
        2,
        blocks={1: ((N, N, 16, 128), lambda i: (0, 0, W_O // 16, 0))},
        flops=2 * TOK * 2048 * COLS,
        size=2_000_000,
    )(exchange(context, "var"), parts)
    return (aggregated, attended)


def solution(mesh):
    return jax.shard_map(
        shards,
        mesh=mesh,
        in_specs=(
            P("var", None, "tok"),
            P("var"),
            P("var", None, None),
            P(),
            P(),
            P(),
            P("tok", "var"),
            P("var", None),
            P(),
            P(None, None, "var"),
            P("var", None),
        ),
        out_specs=(P("tok", "var"), P("tok", "var")),
        check_vma=False,
    )
```

```python
import functools
import math

import jax
import jax.numpy as jnp
from jax import lax
from jax.experimental import pallas as pl
from jax.experimental.pallas import tpu as pltpu
from jax.sharding import PartitionSpec as P

F32 = jnp.float32
BF = jnp.bfloat16
N = 16
SLOTS = 6
TOK = 128
COLS = 256
D = 4096
E = 128
SCALE = 1.0 / math.sqrt(128)

Z = 8
WIDE = 512
PART = 64
PAIRS = 48
ROW_STEP, LEFT_STEP, SUM_STEP = 100, 36, 65


R_U, R_P, R_WH, R_WL, R_M, R_ST, ROWS = 0, 192, 240, 288, 336, 368, 416
W_V, W_P, W_O, W_ROWS = 0, 32, 64, 80


def split2(x):
    hi = x.astype(BF)
    return hi, (x - hi.astype(F32)).astype(BF)


def split3(x):
    hi = x.astype(BF)
    rest = x - hi.astype(F32)
    mid = rest.astype(BF)
    return hi, mid, (rest - mid.astype(F32)).astype(BF)


def call(kernel, out_shape, n_in, scratch=(), smem=(), hbm=(), vmem=16, flops=0, size=0):
    spaces = {i: pltpu.SMEM for i in smem} | {i: pltpu.HBM for i in hbm}
    vm = pl.BlockSpec(memory_space=pltpu.VMEM)
    many = isinstance(out_shape, (tuple, list))
    return pl.pallas_call(
        kernel,
        out_shape=out_shape,
        in_specs=[pl.BlockSpec(memory_space=spaces.get(i, pltpu.VMEM)) for i in range(n_in)],
        out_specs=[vm] * len(out_shape) if many else vm,
        scratch_shapes=list(scratch),
        compiler_params=pltpu.CompilerParams(vmem_limit_bytes=vmem * 1024 * 1024),
        cost_estimate=pl.CostEstimate(flops=flops, bytes_accessed=size, transcendentals=0),
    )


def fetch(parts, row, into, sem):
    copy = pltpu.make_async_copy(parts.at[:, N * row : N * row + into.shape[1]], into, sem)
    copy.start()
    copy.wait()


def weights_kernel(place, value, pool_rows, proj_rows, out):
    half = place[1]
    for v in range(N):
        z = v % Z
        out[v, W_V : W_V + 32] = value[32 * z : 32 * z + 32]
        for x in range(2):
            at = pl.ds(pl.multiple_of(COLS * (Z * x + z) + 128 * half, 128), 128)
            out[v, W_P + 16 * x : W_P + 16 * x + 16] = pool_rows[:, at]
        at = pl.ds(pl.multiple_of(COLS * v + 128 * half, 128), 128)
        out[v, W_O : W_O + 16] = proj_rows[:, at]


def chunks(x, z, j):
    at = [256 * k + 32 * z for k in range(4 * j, 4 * j + 4)]
    return jnp.concatenate([x[:, a : a + 32] for a in at], 1)


def embed_kernel(slot, place, patches, weight, table, gain, keys, out, columns, common):
    wide = table.shape[0]
    row = lax.broadcasted_iota(jnp.int32, (8, wide), 0)
    col = lax.broadcasted_iota(jnp.int32, (8, wide), 1)
    pick = jnp.zeros((8, wide), F32)
    for s in range(SLOTS):
        pick = jnp.where((row == s) & (col == slot[s]), 1.0, pick)
    var_rows = jnp.dot(pick.astype(BF), table[...], preferred_element_type=F32)
    gain_row = gain[...].astype(F32)
    columns[...] = jnp.zeros_like(columns)
    scores = []
    for s in range(SLOTS):
        emb = lax.dot_general(
            patches[s], weight[s], (((0,), (0,)), ((), ())), preferred_element_type=F32
        )
        emb = emb + var_rows[s : s + 1]
        mean = jnp.sum(emb, axis=1, keepdims=True) * (1.0 / D)
        emb = emb - mean
        spread = jnp.sum(emb * emb, axis=1, keepdims=True) * (1.0 / D)
        rstd = lax.rsqrt(spread + 1e-05)
        normed = (emb * rstd * gain_row).astype(BF)
        score = lax.dot_general(
            keys[...], normed, (((1,), (1,)), ((), ())), preferred_element_type=F32
        )
        scores.append(jnp.where(slot[s] >= 0, score * SCALE, -1e30))
        columns[:, s : s + 1] = mean
        columns[:, 6 + s : 7 + s] = rstd
    turned = jnp.transpose(columns[...])
    top = scores[0]
    for s in range(1, SLOTS):
        top = jnp.maximum(top, scores[s])
    weights = [jnp.where(slot[s] >= 0, jnp.exp(scores[s] - top), 0.0) for s in range(SLOTS)]

    def beside(low, high, x):
        at = slice(PART * x, PART * x + PART)
        return jnp.concatenate([low[:, at], high[:, at]], 1)

    tops = [t.astype(F32) for t in split3(top)] + [jnp.zeros((N, TOK), F32)]
    for x in range(2):
        for i in range(3):
            a = 16 * i
            low, high = patches[i].astype(F32), patches[i + 3].astype(F32)
            common[x, a : a + 16] = beside(low, high, x).astype(BF)
            hi, lo = split2(beside(weights[i], weights[i + 3], x))
            common[x, R_WH - R_P + a : R_WH - R_P + a + 16] = hi
            common[x, R_WL - R_P + a : R_WL - R_P + a + 16] = lo
        for i in range(2):
            a = R_M - R_P + 16 * i
            common[x, a : a + 16] = beside(tops[2 * i], tops[2 * i + 1], x).astype(BF)
        stats = []
        for first in (0, 6):
            both = beside(turned[first : first + 3], turned[first + 3 : first + 6], x)
            stats.extend(part.astype(F32) for part in split3(both))
        for z in range(Z):
            out[Z * x + z, R_P:R_ST] = common[x]
            rows = stats + [chunks(var_rows, z, j)[:6] for j in range(4)]
            rows.append(jnp.zeros((6, TOK), F32))
            out[Z * x + z, R_ST:] = jnp.concatenate(rows, 0).astype(BF)
    for i in range(3):
        wide = weight[3 * place[1] + i].astype(F32)
        for z in range(Z):
            for j in range(4):
                a = R_U + 48 * j + 16 * i
                part = chunks(wide, z, j).astype(BF)
                for x in range(2):
                    out[Z * x + z, a : a + 16] = part


def hand_on_kernel(parts, early, out):
    for first, last in ((W_V, W_P), (W_P, W_O), (W_O, W_ROWS)):
        size = last - first
        for h in range(N):
            a = N * first + size * h
            out[a : a + size] = parts[h, first:last]


def pool_kernel(place, got, swapped, gain, summed, weights, turned, rows):
    tops = []
    for v in range(N):
        m = [got[v, R_M + 16 * i : R_M + 16 * i + 16].astype(F32) for i in range(2)]
        tops.append((m[0][:, :PART] + m[0][:, PART:]) + m[1][:, :PART])
    top = tops[0]
    for v in range(1, N):
        top = jnp.maximum(top, tops[v])
    total = jnp.zeros((N, TOK), F32)
    for v in range(N):
        factor = jnp.exp(tops[v] - top)
        factor = jnp.concatenate([factor, factor], 1)
        for i in range(3):
            a = 16 * i
            w = got[v, R_WH + a : R_WH + a + 16].astype(F32) + got[
                v, R_WL + a : R_WL + a + 16
            ].astype(F32)
            w = w * factor
            total = total + w
            weights[48 * v + a : 48 * v + a + 16] = w
    inverse = 1.0 / (total[:, :PART] + total[:, PART:])
    inverse = jnp.concatenate([inverse, inverse], 1)
    odd = lax.broadcasted_iota(jnp.int32, (PAIRS, TOK), 1) % 2 == 1
    for h in range(0, N, 2):
        w = [weights[pl.ds(h + n, PAIRS, stride=16)] * inverse[h + n : h + n + 1] for n in range(2)]
        low = jnp.concatenate([x[:, :PART] for x in w], 1)
        high = jnp.concatenate([x[:, PART:] for x in w], 1)
        gap = jnp.zeros((ROW_STEP - 2 * PAIRS, TOK), F32)
        parts = [jnp.where(odd, 0.0, low), jnp.where(odd, 0.0, high), gap]
        parts += [jnp.where(odd, low, 0.0), jnp.where(odd, high, 0.0)]
        parts.append(jnp.zeros((256 - ROW_STEP - 2 * PAIRS, TOK), F32))
        w = jnp.concatenate(parts, 0)
        for j in range(2):
            part = jnp.transpose(w[128 * j : 128 * j + 128])
            hi = part.astype(BF).astype(F32)
            lo = (part - hi).astype(BF).astype(F32)
            for n in range(2):
                at = slice(PART * n, PART * n + PART)
                turned[j, pl.ds(h + n, PART, stride=LEFT_STEP)] = hi[at]
                turned[j, pl.ds(16 + h + n, PART, stride=LEFT_STEP)] = lo[at]
    gain_row = gain[...].astype(F32)
    even_core = place[1] == 0

    def source(v, carry):
        st = got[v, R_ST:ROWS].astype(F32)
        mean = (st[0:3] + st[3:6]) + st[6:9]
        rstd = (st[9:12] + st[12:15]) + st[15:18]
        both = jnp.transpose(jnp.concatenate([mean, rstd, jnp.zeros((122, TOK), F32)], 0))
        for i in range(3):
            p = got[v, R_P + 16 * i : R_P + 16 * i + 16]
            us = []
            for ref in (got, swapped):
                at = [48 * j + 16 * i for j in range(4)]
                us.append(jnp.concatenate([ref[v, a : a + 16] for a in at], 1))
            sides = (jnp.where(even_core, us[0], us[1]), jnp.where(even_core, us[1], us[0]))
            for n in range(2):
                at = slice(PART * n, PART * n + PART)
                emb = lax.dot_general(
                    p[:, at], sides[n], (((0,), (0,)), ((), ())), preferred_element_type=F32
                )
                col_mean, col_rstd = both[at, i : i + 1], both[at, 3 + i : 4 + i]
                for j in range(4):
                    a = 18 + 6 * j + 3 * n + i
                    x = emb[:, 128 * j : 128 * j + 128] + st[a : a + 1]
                    x = (x - col_mean) * col_rstd * gain_row[:, 128 * j : 128 * j + 128]
                    rows[j, pl.ds(PAIRS * n + 3 * v + i, PART, stride=ROW_STEP)] = x
        return carry

    for j in range(4):
        for i in range(2 * PAIRS, ROW_STEP):
            rows[j, pl.ds(i, PART, stride=ROW_STEP)] = jnp.zeros((PART, 128), F32)
    lax.fori_loop(0, N, source, 0, unroll=4)

    for j in range(2):
        for i in range(32, LEFT_STEP):
            turned[j, pl.ds(i, PART, stride=LEFT_STEP)] = jnp.zeros((PART, 128), F32)

    def two_tokens(g, carry):
        at = pl.ds(pl.multiple_of(g * 2 * LEFT_STEP, 8), 2 * LEFT_STEP)
        lhs = jnp.concatenate([turned[0, at], turned[1, at][:, : 2 * ROW_STEP - 128]], 1)
        span = pl.ds(pl.multiple_of(g * 2 * ROW_STEP, 8), 2 * ROW_STEP)
        rhs = jnp.concatenate([rows[j, span] for j in range(4)], 1)
        y = jnp.dot(lhs.astype(BF), rhs.astype(BF), preferred_element_type=F32)
        for q in range(2):
            a = LEFT_STEP * q
            part = y[a : a + 16] + y[a + 16 : a + 32]
            for j in range(4):
                summed[j, pl.ds(2 * g + q, 16, stride=SUM_STEP)] = part[
                    :, 128 * j : 128 * j + 128
                ]
        return carry

    lax.fori_loop(0, PART // 2, two_tokens, 0, unroll=4)


def values_kernel(summed, parts, out, value, sem):
    fetch(parts, W_V, value, sem)
    for h in range(N):
        at = slice(SUM_STEP * h, SUM_STEP * h + PART)
        hi, lo = split2(jnp.concatenate([summed[j, at] for j in range(4)], 1))
        right = jnp.concatenate([value[k, 32 * h : 32 * h + 32] for k in range(N)], 0)
        whole = jnp.dot(jnp.concatenate([hi, lo], 0), right, preferred_element_type=F32)
        out[h // 2, PART * (h % 2) : PART * (h % 2) + PART] = whole[:PART] + whole[PART:]


def pooled_kernel(got, out):
    total = got[0]
    for z in range(1, Z):
        total = total + got[z]
    total = total.astype(BF)
    for z in range(Z):
        out[z] = total


def columns_of(blocks, weight):
    halves = []
    for half in range(2):
        acc = None
        for h in range(0, N, 2):
            left = jnp.concatenate([blocks[h], blocks[h + 1]], 1)
            right = jnp.concatenate(
                [
                    weight[2 * j + half, a : a + 16]
                    for a in (16 * h, 16 * h + 16)
                    for j in range(8)
                ],
                0,
            )
            term = jnp.dot(left, right, preferred_element_type=F32)
            acc = term if acc is None else acc + term
        halves.append(acc)
    return halves


def state_kernel(got, parts, state, stats, columns, weight, sem):
    fetch(parts, W_P, weight, sem)
    lefts = [jnp.concatenate([got[z, 0:PART], got[z, PART : 2 * PART]], 1) for z in range(Z)]
    total = None
    for c in range(4):
        acc = None
        for z in range(Z):
            right = jnp.concatenate(
                [
                    weight[2 * j + c % 2, a : a + 16]
                    for a in (64 * z + 16 * (c // 2), 64 * z + 32 + 16 * (c // 2))
                    for j in range(8)
                ],
                0,
            )
            term = jnp.dot(lefts[z], right, preferred_element_type=F32)
            acc = term if acc is None else acc + term
        state[:, 128 * c : 128 * c + 128] = acc
        total = acc if total is None else total + acc
    mean = jnp.sum(total, axis=1, keepdims=True) * (1.0 / WIDE)
    spread = jnp.zeros((PART, 128), F32)
    for c in range(4):
        gap = state[:, 128 * c : 128 * c + 128] - mean
        spread = spread + gap * gap
    columns[...] = jnp.zeros_like(columns)
    columns[0:PART, 0:1] = mean
    columns[0:PART, 1:2] = jnp.sum(spread, axis=1, keepdims=True)
    turned = jnp.transpose(columns[...])[0:8]
    for z in range(Z):
        stats[z] = turned


def norm_kernel(got, state, gain, out):
    mean = got[0, 0:1]
    for z in range(1, Z):
        mean = mean + got[z, 0:1]
    mean = mean * (1.0 / Z)
    spread = jnp.zeros((1, TOK), F32)
    for z in range(Z):
        gap = got[z, 0:1] - mean
        spread = spread + (got[z, 1:2] + WIDE * gap * gap)
    rstd = lax.rsqrt(spread * (1.0 / D) + 1e-05)
    both = jnp.transpose(jnp.concatenate([mean, rstd, jnp.zeros((126, TOK), F32)], 0))
    both = both[0:PART]
    normed = ((state[...] - both[:, 0:1]) * both[:, 1:2] * gain[...].astype(F32)).astype(BF)
    for z in range(Z):
        out[z] = normed


def project_kernel(place, own, other, weight, state, query, out, keep, send, whole):
    halves = [
        pl.ds(pl.multiple_of(PART * p, PART), PART) for p in (place[2], 1 - place[2])
    ]
    first = place[2] == 0
    low, high = state[:, 0:COLS].astype(BF), state[:, COLS:].astype(BF)
    keep[...] = jnp.where(first, low, high)
    send[...] = jnp.where(first, high, low)
    for c in range(3):
        acc = None
        for z in range(Z):
            left = jnp.concatenate([own[z], other[z]], 0)
            for x in range(2):
                at = COLS * (Z * x + z)
                term = jnp.dot(
                    left[:, COLS * x : COLS * x + COLS],
                    weight[c, at : at + COLS],
                    preferred_element_type=F32,
                )
                acc = term if acc is None else acc + term
        for i in range(2):
            whole[halves[i]] = acc[PART * i : PART * i + PART]
        result = whole[...].astype(BF)
        if c == 0:
            query[...] = result
        else:
            for k in range(Z):
                out[k, TOK * (c - 1) : TOK * c] = result


def attend_kernel(query, own, other, out, scores):
    q = query[...]
    blocks = [(ref, k) for ref in (own, other) for k in range(Z)]
    peak = None
    for i, (ref, k) in enumerate(blocks):
        s = (
            lax.dot_general(
                q, ref[k, 0:TOK], (((1,), (1,)), ((), ())), preferred_element_type=F32
            )
            * SCALE
        )
        scores[:, TOK * i : TOK * i + TOK] = s
        peak = s if peak is None else jnp.maximum(peak, s)
    peak = jnp.max(peak, axis=1, keepdims=True)
    total, acc = None, None
    for i, (ref, k) in enumerate(blocks):
        e = jnp.exp(scores[:, TOK * i : TOK * i + TOK] - peak)
        total = e if total is None else total + e
        term = jnp.dot(e.astype(BF), ref[k, TOK : 2 * TOK], preferred_element_type=F32)
        acc = term if acc is None else acc + term
    context = (acc / jnp.sum(total, axis=1, keepdims=True)).astype(BF)
    for v in range(N):
        out[v] = context


def output_kernel(place, got, parts, own, other, out, aggregated, weight, sem):
    fetch(parts, W_O, weight, sem)
    halves = columns_of(got, weight)
    for i in range(2):
        out[:, 128 * i : 128 * i + 128] = halves[i].astype(BF)
    for p, ref in ((place[2], own), (1 - place[2], other)):
        aggregated[pl.ds(pl.multiple_of(PART * p, PART), PART)] = ref[...]


def shape(dims, kind):
    return jax.ShapeDtypeStruct(dims, kind)


RINGS = [list(range(Z)), list(range(Z, N))]
CORES = [list(range(0, N, 2)), list(range(1, N, 2))]


def exchange(x, axis, groups=None):
    return lax.all_to_all(x, axis, 0, 0, tiled=True, axis_index_groups=groups)


def swap(x, axis, bits):
    return lax.ppermute(x, axis, [(i, i ^ bits) for i in range(N)])


def shards(
    patches,
    slot_variable,
    embed_weight,
    variable_embed,
    norm_gain,
    pool_keys,
    pool_value,
    pool_out,
    block_gain,
    attend_weight,
    out_proj,
):
    v_idx, k_idx = lax.axis_index("var"), lax.axis_index("tok")
    place = jnp.stack([k_idx // 2, k_idx % 2, v_idx // Z]).astype(jnp.int32)

    rows_of_k = pl.BlockSpec((16, D), lambda i, place: (place[0], 0))
    parts = pl.pallas_call(
        weights_kernel,
        out_shape=shape((N, W_ROWS, 128), BF),
        grid_spec=pltpu.PrefetchScalarGridSpec(
            num_scalar_prefetch=1,
            grid=(1,),
            in_specs=[pl.BlockSpec((COLS, E), lambda i, place: (0, 0)), rows_of_k, rows_of_k],
            out_specs=pl.BlockSpec((N, W_ROWS, 128), lambda i, place: (0, 0, 0)),
        ),
        cost_estimate=pl.CostEstimate(flops=0, bytes_accessed=800_000, transcendentals=0),
    )(place, pool_value, pool_out, out_proj)
    parts = exchange(parts, "var")
    packed = call(
        embed_kernel,
        shape((N, ROWS, 128), BF),
        7,
        (pltpu.VMEM((TOK, 128), F32), pltpu.VMEM((2, R_ST - R_P, TOK), BF)),
        smem=(0, 1),
        flops=2 * SLOTS * TOK * D * 48,
        size=6_000_000,
    )(
        slot_variable,
        place,
        patches,
        embed_weight,
        variable_embed,
        norm_gain[None],
        pool_keys.T,
    )
    parts = call(hand_on_kernel, shape((N * W_ROWS, 128), BF), 2, hbm=(1,), size=600_000)(
        parts, packed
    )
    parts = lax.all_gather(parts, "tok", axis=0)
    got = exchange(packed, "var")
    swapped = swap(got[:, R_U:R_P], "tok", 1)
    gain = lax.dynamic_index_in_dim(norm_gain.reshape(N, Z, 32), v_idx % Z, 1, keepdims=False)

    summed = call(
        pool_kernel,
        shape((4, N * SUM_STEP, 128), F32),
        4,
        (
            pltpu.VMEM((PAIRS * N, TOK), F32),
            pltpu.VMEM((2, PART * LEFT_STEP, TOK), F32),
            pltpu.VMEM((4, PART * ROW_STEP, 128), F32),
        ),
        smem=(0,),
        vmem=26,
        flops=2 * 400_000_000,
        size=5_000_000,
    )(place, got, swapped, gain.reshape(1, WIDE))
    partial = call(
        values_kernel,
        shape((Z, TOK, E), F32),
        2,
        (pltpu.VMEM((N, 32 * N, E), BF), pltpu.SemaphoreType.DMA),
        hbm=(1,),
        vmem=60,
        flops=4 * PART * WIDE * 2048,
        size=5_000_000,
    )(summed, parts)
    pooled = call(pooled_kernel, shape((Z, TOK, E), BF), 1, size=800_000)(
        exchange(partial, "var", RINGS)
    )
    state, stats = call(
        state_kernel,
        (shape((PART, WIDE), F32), shape((Z, 8, 128), F32)),
        2,
        (
            pltpu.VMEM((TOK, 128), F32),
            pltpu.VMEM((N, 32 * N, 128), BF),
            pltpu.SemaphoreType.DMA,
        ),
        hbm=(1,),
        vmem=60,
        flops=2 * PART * 2048 * WIDE,
        size=3_000_000,
    )(exchange(pooled, "var", RINGS), parts)
    gain = lax.dynamic_index_in_dim(block_gain.reshape(2, Z, COLS), v_idx % Z, 1, keepdims=False)
    normed = call(norm_kernel, shape((Z, PART, WIDE), BF), 3, size=700_000)(
        exchange(stats, "var", RINGS), state, gain.reshape(1, WIDE)
    )
    normed = exchange(normed, "var", RINGS)
    query, kv, keep, send = call(
        project_kernel,
        (
            shape((TOK, E), BF),
            shape((Z, 2 * TOK, E), BF),
            shape((PART, COLS), BF),
            shape((PART, COLS), BF),
        ),
        5,
        (pltpu.VMEM((TOK, E), F32),),
        smem=(0,),
        flops=2 * TOK * D * 384,
        size=5_000_000,
    )(place, normed, swap(normed, "var", Z), attend_weight, state)
    kv = exchange(kv, "tok", CORES)
    context = call(
        attend_kernel,
        shape((N, TOK, E), BF),
        3,
        (pltpu.VMEM((TOK, N * TOK), F32),),
        flops=4 * TOK * 2048 * E,
        size=1_500_000,
    )(query, kv, swap(kv, "tok", 1))
    attended, aggregated = call(
        output_kernel,
        (shape((TOK, COLS), BF), shape((TOK, COLS), BF)),
        5,
        (pltpu.VMEM((N, 16 * N, 128), BF), pltpu.SemaphoreType.DMA),
        smem=(0,),
        hbm=(2,),
        vmem=60,
        flops=2 * TOK * 2048 * COLS,
        size=2_000_000,
    )(place, exchange(context, "var"), parts, keep, swap(send, "var", Z))
    return (aggregated, attended)


def solution(mesh):
    return jax.shard_map(
        shards,
        mesh=mesh,
        in_specs=(
            P("var", None, "tok"),
            P("var"),
            P("var", None, None),
            P(),
            P(),
            P(),
            P("tok", "var"),
            P("var", None),
            P(),
            P(None, None, "var"),
            P("var", None),
        ),
        out_specs=(P("tok", "var"), P("tok", "var")),
        check_vma=False,
    )
```

```python
import functools
import math

import jax
import jax.numpy as jnp
from jax import lax
from jax.experimental import pallas as pl
from jax.experimental.pallas import tpu as pltpu
from jax.sharding import PartitionSpec as P

F32 = jnp.float32
BF = jnp.bfloat16
N = 16
SLOTS = 6
TOK = 128
COLS = 256
D = 4096
E = 128
SCALE = 1.0 / math.sqrt(128)

Z = 8
WIDE = 512
PART = 64
PAIRS = 48
ROW_STEP, LEFT_STEP, SUM_STEP = 100, 36, 65


R_U, R_P, R_WH, R_WL, R_M, R_ST, ROWS = 0, 192, 240, 288, 336, 368, 416
W_V, W_P, W_O, W_ROWS = 0, 32, 64, 80


def split2(x):
    hi = x.astype(BF)
    return hi, (x - hi.astype(F32)).astype(BF)


def split3(x):
    hi = x.astype(BF)
    rest = x - hi.astype(F32)
    mid = rest.astype(BF)
    return hi, mid, (rest - mid.astype(F32)).astype(BF)


def call(kernel, out_shape, n_in, scratch=(), smem=(), hbm=(), vmem=16, flops=0, size=0):
    spaces = {i: pltpu.SMEM for i in smem} | {i: pltpu.HBM for i in hbm}
    vm = pl.BlockSpec(memory_space=pltpu.VMEM)
    many = isinstance(out_shape, (tuple, list))
    return pl.pallas_call(
        kernel,
        out_shape=out_shape,
        in_specs=[pl.BlockSpec(memory_space=spaces.get(i, pltpu.VMEM)) for i in range(n_in)],
        out_specs=[vm] * len(out_shape) if many else vm,
        scratch_shapes=list(scratch),
        compiler_params=pltpu.CompilerParams(vmem_limit_bytes=vmem * 1024 * 1024),
        cost_estimate=pl.CostEstimate(flops=flops, bytes_accessed=size, transcendentals=0),
    )


def fetch(parts, row, into, sem):
    copy = pltpu.make_async_copy(parts.at[:, N * row : N * row + into.shape[1]], into, sem)
    copy.start()
    copy.wait()


def weights_kernel(place, value, pool_rows, proj_rows, out):
    half = place[1]
    for v in range(N):
        z = v % Z
        out[v, W_V : W_V + 32] = value[32 * z : 32 * z + 32]
        for x in range(2):
            at = pl.ds(pl.multiple_of(COLS * (Z * x + z) + 128 * half, 128), 128)
            out[v, W_P + 16 * x : W_P + 16 * x + 16] = pool_rows[:, at]
        at = pl.ds(pl.multiple_of(COLS * v + 128 * half, 128), 128)
        out[v, W_O : W_O + 16] = proj_rows[:, at]


def chunks(x, z, j):
    at = [256 * k + 32 * z for k in range(4 * j, 4 * j + 4)]
    return jnp.concatenate([x[:, a : a + 32] for a in at], 1)


def embed_kernel(slot, place, patches, weight, table, gain, keys, out, columns, common):
    wide = table.shape[0]
    row = lax.broadcasted_iota(jnp.int32, (8, wide), 0)
    col = lax.broadcasted_iota(jnp.int32, (8, wide), 1)
    pick = jnp.zeros((8, wide), F32)
    for s in range(SLOTS):
        pick = jnp.where((row == s) & (col == slot[s]), 1.0, pick)
    var_rows = jnp.dot(pick.astype(BF), table[...], preferred_element_type=F32)
    gain_row = gain[...].astype(F32)
    columns[...] = jnp.zeros_like(columns)
    scores = []
    for s in range(SLOTS):
        emb = lax.dot_general(
            patches[s], weight[s], (((0,), (0,)), ((), ())), preferred_element_type=F32
        )
        emb = emb + var_rows[s : s + 1]
        mean = jnp.sum(emb, axis=1, keepdims=True) * (1.0 / D)
        emb = emb - mean
        spread = jnp.sum(emb * emb, axis=1, keepdims=True) * (1.0 / D)
        rstd = lax.rsqrt(spread + 1e-05)
        normed = (emb * rstd * gain_row).astype(BF)
        score = lax.dot_general(
            keys[...], normed, (((1,), (1,)), ((), ())), preferred_element_type=F32
        )
        scores.append(jnp.where(slot[s] >= 0, score * SCALE, -1e30))
        columns[:, s : s + 1] = mean
        columns[:, 6 + s : 7 + s] = rstd
    turned = jnp.transpose(columns[...])
    top = scores[0]
    for s in range(1, SLOTS):
        top = jnp.maximum(top, scores[s])
    weights = [jnp.where(slot[s] >= 0, jnp.exp(scores[s] - top), 0.0) for s in range(SLOTS)]

    def beside(low, high, x):
        at = slice(PART * x, PART * x + PART)
        return jnp.concatenate([low[:, at], high[:, at]], 1)

    tops = [t.astype(F32) for t in split3(top)] + [jnp.zeros((N, TOK), F32)]
    for x in range(2):
        for i in range(3):
            a = 16 * i
            low, high = patches[i].astype(F32), patches[i + 3].astype(F32)
            common[x, a : a + 16] = beside(low, high, x).astype(BF)
            hi, lo = split2(beside(weights[i], weights[i + 3], x))
            common[x, R_WH - R_P + a : R_WH - R_P + a + 16] = hi
            common[x, R_WL - R_P + a : R_WL - R_P + a + 16] = lo
        for i in range(2):
            a = R_M - R_P + 16 * i
            common[x, a : a + 16] = beside(tops[2 * i], tops[2 * i + 1], x).astype(BF)
        stats = []
        for first in (0, 6):
            both = beside(turned[first : first + 3], turned[first + 3 : first + 6], x)
            stats.extend(part.astype(F32) for part in split3(both))
        for z in range(Z):
            out[Z * x + z, R_P:R_ST] = common[x]
            rows = stats + [chunks(var_rows, z, j)[:6] for j in range(4)]
            rows.append(jnp.zeros((6, TOK), F32))
            out[Z * x + z, R_ST:] = jnp.concatenate(rows, 0).astype(BF)
    for i in range(3):
        wide = weight[3 * place[1] + i].astype(F32)
        for z in range(Z):
            for j in range(4):
                a = R_U + 48 * j + 16 * i
                part = chunks(wide, z, j).astype(BF)
                for x in range(2):
                    out[Z * x + z, a : a + 16] = part


def hand_on_kernel(parts, early, out):
    for first, last in ((W_V, W_P), (W_P, W_O), (W_O, W_ROWS)):
        size = last - first
        for h in range(N):
            a = N * first + size * h
            out[a : a + size] = parts[h, first:last]


def pool_kernel(place, got, swapped, gain, summed, weights, turned, rows):
    tops = []
    for v in range(N):
        m = [got[v, R_M + 16 * i : R_M + 16 * i + 16].astype(F32) for i in range(2)]
        tops.append((m[0][:, :PART] + m[0][:, PART:]) + m[1][:, :PART])
    top = tops[0]
    for v in range(1, N):
        top = jnp.maximum(top, tops[v])
    total = jnp.zeros((N, TOK), F32)
    for v in range(N):
        factor = jnp.exp(tops[v] - top)
        factor = jnp.concatenate([factor, factor], 1)
        for i in range(3):
            a = 16 * i
            w = got[v, R_WH + a : R_WH + a + 16].astype(F32) + got[
                v, R_WL + a : R_WL + a + 16
            ].astype(F32)
            w = w * factor
            total = total + w
            weights[48 * v + a : 48 * v + a + 16] = w
    inverse = 1.0 / (total[:, :PART] + total[:, PART:])
    inverse = jnp.concatenate([inverse, inverse], 1)
    odd = lax.broadcasted_iota(jnp.int32, (PAIRS, TOK), 1) % 2 == 1
    for h in range(0, N, 2):
        w = [weights[pl.ds(h + n, PAIRS, stride=16)] * inverse[h + n : h + n + 1] for n in range(2)]
        low = jnp.concatenate([x[:, :PART] for x in w], 1)
        high = jnp.concatenate([x[:, PART:] for x in w], 1)
        gap = jnp.zeros((ROW_STEP - 2 * PAIRS, TOK), F32)
        parts = [jnp.where(odd, 0.0, low), jnp.where(odd, 0.0, high), gap]
        parts += [jnp.where(odd, low, 0.0), jnp.where(odd, high, 0.0)]
        parts.append(jnp.zeros((256 - ROW_STEP - 2 * PAIRS, TOK), F32))
        w = jnp.concatenate(parts, 0)
        for j in range(2):
            part = jnp.transpose(w[128 * j : 128 * j + 128])
            hi = part.astype(BF).astype(F32)
            lo = (part - hi).astype(BF).astype(F32)
            for n in range(2):
                at = slice(PART * n, PART * n + PART)
                turned[j, pl.ds(h + n, PART, stride=LEFT_STEP)] = hi[at]
                turned[j, pl.ds(16 + h + n, PART, stride=LEFT_STEP)] = lo[at]
    gain_row = gain[...].astype(F32)
    even_core = place[1] == 0

    def source(v, carry):
        st = got[v, R_ST:ROWS].astype(F32)
        mean = (st[0:3] + st[3:6]) + st[6:9]
        rstd = (st[9:12] + st[12:15]) + st[15:18]
        both = jnp.transpose(jnp.concatenate([mean, rstd, jnp.zeros((122, TOK), F32)], 0))
        for i in range(3):
            p = got[v, R_P + 16 * i : R_P + 16 * i + 16]
            us = []
            for ref in (got, swapped):
                at = [48 * j + 16 * i for j in range(4)]
                us.append(jnp.concatenate([ref[v, a : a + 16] for a in at], 1))
            sides = (jnp.where(even_core, us[0], us[1]), jnp.where(even_core, us[1], us[0]))
            for n in range(2):
                at = slice(PART * n, PART * n + PART)
                emb = lax.dot_general(
                    p[:, at], sides[n], (((0,), (0,)), ((), ())), preferred_element_type=F32
                )
                col_mean, col_rstd = both[at, i : i + 1], both[at, 3 + i : 4 + i]
                for j in range(4):
                    a = 18 + 6 * j + 3 * n + i
                    x = emb[:, 128 * j : 128 * j + 128] + st[a : a + 1]
                    x = (x - col_mean) * col_rstd * gain_row[:, 128 * j : 128 * j + 128]
                    rows[j, pl.ds(PAIRS * n + 3 * v + i, PART, stride=ROW_STEP)] = x
        return carry

    for j in range(4):
        for i in range(2 * PAIRS, ROW_STEP):
            rows[j, pl.ds(i, PART, stride=ROW_STEP)] = jnp.zeros((PART, 128), F32)
    lax.fori_loop(0, N, source, 0, unroll=4)

    for j in range(2):
        for i in range(32, LEFT_STEP):
            turned[j, pl.ds(i, PART, stride=LEFT_STEP)] = jnp.zeros((PART, 128), F32)

    def two_tokens(g, carry):
        at = pl.ds(pl.multiple_of(g * 2 * LEFT_STEP, 8), 2 * LEFT_STEP)
        lhs = jnp.concatenate([turned[0, at], turned[1, at][:, : 2 * ROW_STEP - 128]], 1)
        span = pl.ds(pl.multiple_of(g * 2 * ROW_STEP, 8), 2 * ROW_STEP)
        rhs = jnp.concatenate([rows[j, span] for j in range(4)], 1)
        y = jnp.dot(lhs.astype(BF), rhs.astype(BF), preferred_element_type=F32)
        for q in range(2):
            a = LEFT_STEP * q
            part = y[a : a + 16] + y[a + 16 : a + 32]
            for j in range(4):
                summed[j, pl.ds(2 * g + q, 16, stride=SUM_STEP)] = part[
                    :, 128 * j : 128 * j + 128
                ]
        return carry

    lax.fori_loop(0, PART // 2, two_tokens, 0, unroll=4)


def values_kernel(summed, parts, out, value, sem):
    fetch(parts, W_V, value, sem)
    for h in range(N):
        at = slice(SUM_STEP * h, SUM_STEP * h + PART)
        hi, lo = split2(jnp.concatenate([summed[j, at] for j in range(4)], 1))
        right = jnp.concatenate([value[k, 32 * h : 32 * h + 32] for k in range(N)], 0)
        whole = jnp.dot(jnp.concatenate([hi, lo], 0), right, preferred_element_type=F32)
        out[h // 2, PART * (h % 2) : PART * (h % 2) + PART] = whole[:PART] + whole[PART:]


def pooled_kernel(got, out):
    total = got[0]
    for z in range(1, Z):
        total = total + got[z]
    total = total.astype(BF)
    for z in range(Z):
        out[z] = total


def columns_of(blocks, weight):
    halves = []
    for half in range(2):
        acc = None
        for h in range(0, N, 2):
            left = jnp.concatenate([blocks[h], blocks[h + 1]], 1)
            right = jnp.concatenate(
                [
                    weight[2 * j + half, a : a + 16]
                    for a in (16 * h, 16 * h + 16)
                    for j in range(8)
                ],
                0,
            )
            term = jnp.dot(left, right, preferred_element_type=F32)
            acc = term if acc is None else acc + term
        halves.append(acc)
    return halves


def state_kernel(got, parts, state, stats, columns, weight, sem):
    fetch(parts, W_P, weight, sem)
    lefts = [jnp.concatenate([got[z, 0:PART], got[z, PART : 2 * PART]], 1) for z in range(Z)]
    total = None
    for c in range(4):
        acc = None
        for z in range(Z):
            right = jnp.concatenate(
                [
                    weight[2 * j + c % 2, a : a + 16]
                    for a in (64 * z + 16 * (c // 2), 64 * z + 32 + 16 * (c // 2))
                    for j in range(8)
                ],
                0,
            )
            term = jnp.dot(lefts[z], right, preferred_element_type=F32)
            acc = term if acc is None else acc + term
        state[:, 128 * c : 128 * c + 128] = acc
        total = acc if total is None else total + acc
    mean = jnp.sum(total, axis=1, keepdims=True) * (1.0 / WIDE)
    spread = jnp.zeros((PART, 128), F32)
    for c in range(4):
        gap = state[:, 128 * c : 128 * c + 128] - mean
        spread = spread + gap * gap
    columns[...] = jnp.zeros_like(columns)
    columns[0:PART, 0:1] = mean
    columns[0:PART, 1:2] = jnp.sum(spread, axis=1, keepdims=True)
    turned = jnp.transpose(columns[...])[0:8]
    for z in range(Z):
        stats[z] = turned


def norm_kernel(got, state, gain, out):
    mean = got[0, 0:1]
    for z in range(1, Z):
        mean = mean + got[z, 0:1]
    mean = mean * (1.0 / Z)
    spread = jnp.zeros((1, TOK), F32)
    for z in range(Z):
        gap = got[z, 0:1] - mean
        spread = spread + (got[z, 1:2] + WIDE * gap * gap)
    rstd = lax.rsqrt(spread * (1.0 / D) + 1e-05)
    both = jnp.transpose(jnp.concatenate([mean, rstd, jnp.zeros((126, TOK), F32)], 0))
    both = both[0:PART]
    normed = ((state[...] - both[:, 0:1]) * both[:, 1:2] * gain[...].astype(F32)).astype(BF)
    for z in range(Z):
        out[z] = normed


def project_kernel(place, own, other, weight, state, query, out, keep, send, whole):
    halves = [
        pl.ds(pl.multiple_of(PART * p, PART), PART) for p in (place[2], 1 - place[2])
    ]
    first = place[2] == 0
    low, high = state[:, 0:COLS].astype(BF), state[:, COLS:].astype(BF)
    keep[...] = jnp.where(first, low, high)
    send[...] = jnp.where(first, high, low)
    for c in range(3):
        acc = None
        for z in range(Z):
            left = jnp.concatenate([own[z], other[z]], 0)
            for x in range(2):
                at = COLS * (Z * x + z)
                term = jnp.dot(
                    left[:, COLS * x : COLS * x + COLS],
                    weight[c, at : at + COLS],
                    preferred_element_type=F32,
                )
                acc = term if acc is None else acc + term
        for i in range(2):
            whole[halves[i]] = acc[PART * i : PART * i + PART]
        result = whole[...].astype(BF)
        if c == 0:
            query[...] = result
        else:
            for k in range(Z):
                out[k, TOK * (c - 1) : TOK * c] = result


def attend_kernel(query, own, other, out, scores):
    q = query[...]
    blocks = [(ref, k) for ref in (own, other) for k in range(Z)]
    peak = None
    for i, (ref, k) in enumerate(blocks):
        s = (
            lax.dot_general(
                q, ref[k, 0:TOK], (((1,), (1,)), ((), ())), preferred_element_type=F32
            )
            * SCALE
        )
        scores[:, TOK * i : TOK * i + TOK] = s
        peak = s if peak is None else jnp.maximum(peak, s)
    peak = jnp.max(peak, axis=1, keepdims=True)
    total, acc = None, None
    for i, (ref, k) in enumerate(blocks):
        e = jnp.exp(scores[:, TOK * i : TOK * i + TOK] - peak)
        total = e if total is None else total + e
        term = jnp.dot(e.astype(BF), ref[k, TOK : 2 * TOK], preferred_element_type=F32)
        acc = term if acc is None else acc + term
    context = (acc / jnp.sum(total, axis=1, keepdims=True)).astype(BF)
    for v in range(N):
        out[v] = context


def output_kernel(place, got, parts, own, other, out, aggregated, weight, sem):
    fetch(parts, W_O, weight, sem)
    halves = columns_of(got, weight)
    for i in range(2):
        out[:, 128 * i : 128 * i + 128] = halves[i].astype(BF)
    for p, ref in ((place[2], own), (1 - place[2], other)):
        aggregated[pl.ds(pl.multiple_of(PART * p, PART), PART)] = ref[...]


def shape(dims, kind):
    return jax.ShapeDtypeStruct(dims, kind)


RINGS = [list(range(Z)), list(range(Z, N))]
CORES = [list(range(0, N, 2)), list(range(1, N, 2))]


def exchange(x, axis, groups=None):
    return lax.all_to_all(x, axis, 0, 0, tiled=True, axis_index_groups=groups)


def swap(x, axis, bits):
    return lax.ppermute(x, axis, [(i, i ^ bits) for i in range(N)])


def shards(
    patches,
    slot_variable,
    embed_weight,
    variable_embed,
    norm_gain,
    pool_keys,
    pool_value,
    pool_out,
    block_gain,
    attend_weight,
    out_proj,
):
    v_idx, k_idx = lax.axis_index("var"), lax.axis_index("tok")
    place = jnp.stack([k_idx // 2, k_idx % 2, v_idx // Z]).astype(jnp.int32)

    rows_of_k = pl.BlockSpec((16, D), lambda i, place: (place[0], 0))
    parts = pl.pallas_call(
        weights_kernel,
        out_shape=shape((N, W_ROWS, 128), BF),
        grid_spec=pltpu.PrefetchScalarGridSpec(
            num_scalar_prefetch=1,
            grid=(1,),
            in_specs=[pl.BlockSpec((COLS, E), lambda i, place: (0, 0)), rows_of_k, rows_of_k],
            out_specs=pl.BlockSpec((N, W_ROWS, 128), lambda i, place: (0, 0, 0)),
        ),
        cost_estimate=pl.CostEstimate(flops=0, bytes_accessed=800_000, transcendentals=0),
    )(place, pool_value, pool_out, out_proj)
    parts = exchange(parts, "var")
    packed = call(
        embed_kernel,
        shape((N, ROWS, 128), BF),
        7,
        (pltpu.VMEM((TOK, 128), F32), pltpu.VMEM((2, R_ST - R_P, TOK), BF)),
        smem=(0, 1),
        flops=2 * SLOTS * TOK * D * 48,
        size=6_000_000,
    )(
        slot_variable,
        place,
        patches,
        embed_weight,
        variable_embed,
        norm_gain[None],
        pool_keys.T,
    )
    parts = call(hand_on_kernel, shape((N * W_ROWS, 128), BF), 2, hbm=(1,), size=600_000)(
        parts, packed
    )
    parts = lax.all_gather(parts, "tok", axis=0)
    got = exchange(packed, "var")
    swapped = swap(got[:, R_U:R_P], "tok", 1)
    gain = lax.dynamic_index_in_dim(norm_gain.reshape(N, Z, 32), v_idx % Z, 1, keepdims=False)

    summed = call(
        pool_kernel,
        shape((4, N * SUM_STEP, 128), F32),
        4,
        (
            pltpu.VMEM((PAIRS * N, TOK), F32),
            pltpu.VMEM((2, PART * LEFT_STEP, TOK), F32),
            pltpu.VMEM((4, PART * ROW_STEP, 128), F32),
        ),
        smem=(0,),
        vmem=26,
        flops=2 * 400_000_000,
        size=5_000_000,
    )(place, got, swapped, gain.reshape(1, WIDE))
    partial = call(
        values_kernel,
        shape((Z, TOK, E), F32),
        2,
        (pltpu.VMEM((N, 32 * N, E), BF), pltpu.SemaphoreType.DMA),
        hbm=(1,),
        vmem=16,
        flops=4 * PART * WIDE * 2048,
        size=5_000_000,
    )(summed, parts)
    pooled = call(pooled_kernel, shape((Z, TOK, E), BF), 1, size=800_000)(
        exchange(partial, "var", RINGS)
    )
    state, stats = call(
        state_kernel,
        (shape((PART, WIDE), F32), shape((Z, 8, 128), F32)),
        2,
        (
            pltpu.VMEM((TOK, 128), F32),
            pltpu.VMEM((N, 32 * N, 128), BF),
            pltpu.SemaphoreType.DMA,
        ),
        hbm=(1,),
        vmem=16,
        flops=2 * PART * 2048 * WIDE,
        size=3_000_000,
    )(exchange(pooled, "var", RINGS), parts)
    gain = lax.dynamic_index_in_dim(block_gain.reshape(2, Z, COLS), v_idx % Z, 1, keepdims=False)
    normed = call(norm_kernel, shape((Z, PART, WIDE), BF), 3, size=700_000)(
        exchange(stats, "var", RINGS), state, gain.reshape(1, WIDE)
    )
    normed = exchange(normed, "var", RINGS)
    query, kv, keep, send = call(
        project_kernel,
        (
            shape((TOK, E), BF),
            shape((Z, 2 * TOK, E), BF),
            shape((PART, COLS), BF),
            shape((PART, COLS), BF),
        ),
        5,
        (pltpu.VMEM((TOK, E), F32),),
        smem=(0,),
        flops=2 * TOK * D * 384,
        size=5_000_000,
    )(place, normed, swap(normed, "var", Z), attend_weight, state)
    kv = exchange(kv, "tok", CORES)
    context = call(
        attend_kernel,
        shape((N, TOK, E), BF),
        3,
        (pltpu.VMEM((TOK, N * TOK), F32),),
        flops=4 * TOK * 2048 * E,
        size=1_500_000,
    )(query, kv, swap(kv, "tok", 1))
    attended, aggregated = call(
        output_kernel,
        (shape((TOK, COLS), BF), shape((TOK, COLS), BF)),
        5,
        (pltpu.VMEM((N, 16 * N, 128), BF), pltpu.SemaphoreType.DMA),
        smem=(0,),
        hbm=(2,),
        vmem=16,
        flops=2 * TOK * 2048 * COLS,
        size=2_000_000,
    )(place, exchange(context, "var"), parts, keep, swap(send, "var", Z))
    return (aggregated, attended)


def solution(mesh):
    return jax.shard_map(
        shards,
        mesh=mesh,
        in_specs=(
            P("var", None, "tok"),
            P("var"),
            P("var", None, None),
            P(),
            P(),
            P(),
            P("tok", "var"),
            P("var", None),
            P(),
            P(None, None, "var"),
            P("var", None),
        ),
        out_specs=(P("tok", "var"), P("tok", "var")),
        check_vma=False,
    )
```

```python
import functools
import math

import jax
import jax.numpy as jnp
from jax import lax
from jax.experimental import pallas as pl
from jax.experimental.pallas import tpu as pltpu
from jax.sharding import PartitionSpec as P

F32 = jnp.float32
BF = jnp.bfloat16
N = 16
SLOTS = 6
TOK = 128
COLS = 256
D = 4096
E = 128
SCALE = 1.0 / math.sqrt(128)

Z = 8
WIDE = 512
PART = 64
PAIRS = 48
ROW_STEP, LEFT_STEP, SUM_STEP = 100, 36, 65


R_U, R_P, R_WH, R_WL, R_M, R_ST, ROWS = 0, 192, 240, 288, 336, 368, 416
W_V, W_P, W_O, W_ROWS = 0, 32, 48, 64


def split2(x):
    hi = x.astype(BF)
    return hi, (x - hi.astype(F32)).astype(BF)


def split3(x):
    hi = x.astype(BF)
    rest = x - hi.astype(F32)
    mid = rest.astype(BF)
    return hi, mid, (rest - mid.astype(F32)).astype(BF)


def call(kernel, out_shape, n_in, scratch=(), smem=(), hbm=(), vmem=16, flops=0, size=0):
    spaces = {i: pltpu.SMEM for i in smem} | {i: pltpu.HBM for i in hbm}
    vm = pl.BlockSpec(memory_space=pltpu.VMEM)
    many = isinstance(out_shape, (tuple, list))
    return pl.pallas_call(
        kernel,
        out_shape=out_shape,
        in_specs=[pl.BlockSpec(memory_space=spaces.get(i, pltpu.VMEM)) for i in range(n_in)],
        out_specs=[vm] * len(out_shape) if many else vm,
        scratch_shapes=list(scratch),
        compiler_params=pltpu.CompilerParams(vmem_limit_bytes=vmem * 1024 * 1024),
        cost_estimate=pl.CostEstimate(flops=flops, bytes_accessed=size, transcendentals=0),
    )


def weights_kernel(place, value, pool_rows, proj_rows, out):
    half = place[1]
    for v in range(N):
        z = v % Z
        out[v, W_V : W_V + 32] = value[32 * z : 32 * z + 32]
        at = pl.ds(pl.multiple_of(COLS * v + 128 * half, 128), 128)
        out[v, W_P : W_P + 16] = pool_rows[:, at]
        out[v, W_O : W_O + 16] = proj_rows[:, at]


def chunks(x, z, j):
    at = [256 * k + 32 * z for k in range(4 * j, 4 * j + 4)]
    return jnp.concatenate([x[:, a : a + 32] for a in at], 1)


def embed_kernel(slot, place, patches, weight, table, gain, keys, out, columns, common):
    wide = table.shape[0]
    row = lax.broadcasted_iota(jnp.int32, (8, wide), 0)
    col = lax.broadcasted_iota(jnp.int32, (8, wide), 1)
    pick = jnp.zeros((8, wide), F32)
    for s in range(SLOTS):
        pick = jnp.where((row == s) & (col == slot[s]), 1.0, pick)
    var_rows = jnp.dot(pick.astype(BF), table[...], preferred_element_type=F32)
    gain_row = gain[...].astype(F32)
    columns[...] = jnp.zeros_like(columns)
    scores = []
    for s in range(SLOTS):
        emb = lax.dot_general(
            patches[s], weight[s], (((0,), (0,)), ((), ())), preferred_element_type=F32
        )
        emb = emb + var_rows[s : s + 1]
        mean = jnp.sum(emb, axis=1, keepdims=True) * (1.0 / D)
        emb = emb - mean
        spread = jnp.sum(emb * emb, axis=1, keepdims=True) * (1.0 / D)
        rstd = lax.rsqrt(spread + 1e-05)
        normed = (emb * rstd * gain_row).astype(BF)
        score = lax.dot_general(
            keys[...], normed, (((1,), (1,)), ((), ())), preferred_element_type=F32
        )
        scores.append(jnp.where(slot[s] >= 0, score * SCALE, -1e30))
        columns[:, s : s + 1] = mean
        columns[:, 6 + s : 7 + s] = rstd
    turned = jnp.transpose(columns[...])
    top = scores[0]
    for s in range(1, SLOTS):
        top = jnp.maximum(top, scores[s])
    weights = [jnp.where(slot[s] >= 0, jnp.exp(scores[s] - top), 0.0) for s in range(SLOTS)]

    def beside(low, high, x):
        at = slice(PART * x, PART * x + PART)
        return jnp.concatenate([low[:, at], high[:, at]], 1)

    tops = [t.astype(F32) for t in split3(top)] + [jnp.zeros((N, TOK), F32)]
    for x in range(2):
        for i in range(3):
            a = 16 * i
            low, high = patches[i].astype(F32), patches[i + 3].astype(F32)
            common[x, a : a + 16] = beside(low, high, x).astype(BF)
            hi, lo = split2(beside(weights[i], weights[i + 3], x))
            common[x, R_WH - R_P + a : R_WH - R_P + a + 16] = hi
            common[x, R_WL - R_P + a : R_WL - R_P + a + 16] = lo
        for i in range(2):
            a = R_M - R_P + 16 * i
            common[x, a : a + 16] = beside(tops[2 * i], tops[2 * i + 1], x).astype(BF)
        stats = []
        for first in (0, 6):
            both = beside(turned[first : first + 3], turned[first + 3 : first + 6], x)
            stats.extend(part.astype(F32) for part in split3(both))
        for z in range(Z):
            out[Z * x + z, R_P:R_ST] = common[x]
            rows = stats + [chunks(var_rows, z, j)[:6] for j in range(4)]
            rows.append(jnp.zeros((6, TOK), F32))
            out[Z * x + z, R_ST:] = jnp.concatenate(rows, 0).astype(BF)
    for i in range(3):
        wide = weight[3 * place[1] + i].astype(F32)
        for z in range(Z):
            for j in range(4):
                a = R_U + 48 * j + 16 * i
                part = chunks(wide, z, j).astype(BF)
                for x in range(2):
                    out[Z * x + z, a : a + 16] = part


def hand_on_kernel(parts, early, out):
    for first, last in ((W_V, W_P), (W_P, W_O), (W_O, W_ROWS)):
        size = last - first
        for h in range(N):
            a = N * first + size * h
            out[a : a + size] = parts[h, first:last]


def pool_kernel(place, got, swapped, gain, summed, weights, turned, rows):
    tops = []
    for v in range(N):
        m = [got[v, R_M + 16 * i : R_M + 16 * i + 16].astype(F32) for i in range(2)]
        tops.append((m[0][:, :PART] + m[0][:, PART:]) + m[1][:, :PART])
    top = tops[0]
    for v in range(1, N):
        top = jnp.maximum(top, tops[v])
    total = jnp.zeros((N, TOK), F32)
    for v in range(N):
        factor = jnp.exp(tops[v] - top)
        factor = jnp.concatenate([factor, factor], 1)
        for i in range(3):
            a = 16 * i
            w = got[v, R_WH + a : R_WH + a + 16].astype(F32) + got[
                v, R_WL + a : R_WL + a + 16
            ].astype(F32)
            w = w * factor
            total = total + w
            weights[48 * v + a : 48 * v + a + 16] = w
    inverse = 1.0 / (total[:, :PART] + total[:, PART:])
    inverse = jnp.concatenate([inverse, inverse], 1)
    odd = lax.broadcasted_iota(jnp.int32, (PAIRS, TOK), 1) % 2 == 1
    for h in range(0, N, 2):
        w = [weights[pl.ds(h + n, PAIRS, stride=16)] * inverse[h + n : h + n + 1] for n in range(2)]
        low = jnp.concatenate([x[:, :PART] for x in w], 1)
        high = jnp.concatenate([x[:, PART:] for x in w], 1)
        gap = jnp.zeros((ROW_STEP - 2 * PAIRS, TOK), F32)
        parts = [jnp.where(odd, 0.0, low), jnp.where(odd, 0.0, high), gap]
        parts += [jnp.where(odd, low, 0.0), jnp.where(odd, high, 0.0)]
        parts.append(jnp.zeros((256 - ROW_STEP - 2 * PAIRS, TOK), F32))
        w = jnp.concatenate(parts, 0)
        for j in range(2):
            part = jnp.transpose(w[128 * j : 128 * j + 128])
            hi = part.astype(BF).astype(F32)
            lo = (part - hi).astype(BF).astype(F32)
            for n in range(2):
                at = slice(PART * n, PART * n + PART)
                turned[j, pl.ds(h + n, PART, stride=LEFT_STEP)] = hi[at]
                turned[j, pl.ds(16 + h + n, PART, stride=LEFT_STEP)] = lo[at]
    gain_row = gain[...].astype(F32)
    even_core = place[1] == 0

    def source(v, carry):
        st = got[v, R_ST:ROWS].astype(F32)
        mean = (st[0:3] + st[3:6]) + st[6:9]
        rstd = (st[9:12] + st[12:15]) + st[15:18]
        both = jnp.transpose(jnp.concatenate([mean, rstd, jnp.zeros((122, TOK), F32)], 0))
        for i in range(3):
            p = got[v, R_P + 16 * i : R_P + 16 * i + 16]
            us = []
            for ref in (got, swapped):
                at = [48 * j + 16 * i for j in range(4)]
                us.append(jnp.concatenate([ref[v, a : a + 16] for a in at], 1))
            sides = (jnp.where(even_core, us[0], us[1]), jnp.where(even_core, us[1], us[0]))
            for n in range(2):
                at = slice(PART * n, PART * n + PART)
                emb = lax.dot_general(
                    p[:, at], sides[n], (((0,), (0,)), ((), ())), preferred_element_type=F32
                )
                col_mean, col_rstd = both[at, i : i + 1], both[at, 3 + i : 4 + i]
                for j in range(4):
                    a = 18 + 6 * j + 3 * n + i
                    x = emb[:, 128 * j : 128 * j + 128] + st[a : a + 1]
                    x = (x - col_mean) * col_rstd * gain_row[:, 128 * j : 128 * j + 128]
                    rows[j, pl.ds(PAIRS * n + 3 * v + i, PART, stride=ROW_STEP)] = x
        return carry

    for j in range(4):
        for i in range(2 * PAIRS, ROW_STEP):
            rows[j, pl.ds(i, PART, stride=ROW_STEP)] = jnp.zeros((PART, 128), F32)
    lax.fori_loop(0, N, source, 0, unroll=4)

    for j in range(2):
        for i in range(32, LEFT_STEP):
            turned[j, pl.ds(i, PART, stride=LEFT_STEP)] = jnp.zeros((PART, 128), F32)

    def two_tokens(g, carry):
        at = pl.ds(pl.multiple_of(g * 2 * LEFT_STEP, 8), 2 * LEFT_STEP)
        lhs = jnp.concatenate([turned[0, at], turned[1, at][:, : 2 * ROW_STEP - 128]], 1)
        span = pl.ds(pl.multiple_of(g * 2 * ROW_STEP, 8), 2 * ROW_STEP)
        rhs = jnp.concatenate([rows[j, span] for j in range(4)], 1)
        y = jnp.dot(lhs.astype(BF), rhs.astype(BF), preferred_element_type=F32)
        for q in range(2):
            a = LEFT_STEP * q
            part = y[a : a + 16] + y[a + 16 : a + 32]
            for j in range(4):
                summed[j, pl.ds(2 * g + q, 16, stride=SUM_STEP)] = part[
                    :, 128 * j : 128 * j + 128
                ]
        return carry

    lax.fori_loop(0, PART // 2, two_tokens, 0, unroll=4)


def values_kernel(summed, parts, out, pool_part, proj_part, value, sems):
    copies = []
    for i, (row, into) in enumerate(((W_V, value), (W_P, pool_part), (W_O, proj_part))):
        span = pl.ds(N * row, into.shape[1])
        copies.append(pltpu.make_async_copy(parts.at[:, span], into, sems.at[i]))
    for copy in copies:
        copy.start()
    copies[0].wait()
    for h in range(N):
        at = slice(SUM_STEP * h, SUM_STEP * h + PART)
        hi, lo = split2(jnp.concatenate([summed[j, at] for j in range(4)], 1))
        right = jnp.concatenate([value[k, 32 * h : 32 * h + 32] for k in range(N)], 0)
        whole = jnp.dot(jnp.concatenate([hi, lo], 0), right, preferred_element_type=F32)
        out[h // 2, PART * (h % 2) : PART * (h % 2) + PART] = whole[:PART] + whole[PART:]
    for copy in copies[1:]:
        copy.wait()


def pooled_kernel(got, out):
    total = got[0]
    for z in range(1, Z):
        total = total + got[z]
    total = total.astype(BF)
    for v in range(N):
        out[v] = total


def columns_of(pairs, weight):
    halves = []
    for half in range(2):
        acc = None
        for i, left in enumerate(pairs):
            right = jnp.concatenate(
                [
                    weight[2 * j + half, a : a + 16]
                    for a in (32 * i, 32 * i + 16)
                    for j in range(8)
                ],
                0,
            )
            term = jnp.dot(left, right, preferred_element_type=F32)
            acc = term if acc is None else acc + term
        halves.append(acc)
    return halves


def state_kernel(got, weight, state, aggregated, stats, columns):
    pairs = []
    for z in range(Z):
        sides = [
            jnp.concatenate([got[v, 0:PART], got[v, PART : 2 * PART]], 1) for v in (z, Z + z)
        ]
        pairs.append(jnp.concatenate(sides, 0))
    halves = columns_of(pairs, weight)
    mean = jnp.sum(halves[0] + halves[1], axis=1, keepdims=True) * (1.0 / COLS)
    spread = jnp.zeros((TOK, 128), F32)
    for i in range(2):
        state[:, 128 * i : 128 * i + 128] = halves[i]
        aggregated[:, 128 * i : 128 * i + 128] = halves[i].astype(BF)
        gap = halves[i] - mean
        spread = spread + gap * gap
    columns[...] = jnp.zeros_like(columns)
    columns[:, 0:1] = mean
    columns[:, 1:2] = jnp.sum(spread, axis=1, keepdims=True)
    turned = jnp.transpose(columns[...])[0:8]
    for v in range(N):
        stats[v] = turned


def norm_kernel(got, state, gain, out):
    mean = got[0, 0:1]
    for v in range(1, N):
        mean = mean + got[v, 0:1]
    mean = mean * (1.0 / N)
    spread = jnp.zeros((1, TOK), F32)
    for v in range(N):
        gap = got[v, 0:1] - mean
        spread = spread + (got[v, 1:2] + COLS * gap * gap)
    rstd = lax.rsqrt(spread * (1.0 / D) + 1e-05)
    both = jnp.transpose(jnp.concatenate([mean, rstd, jnp.zeros((126, TOK), F32)], 0))
    normed = ((state[...] - both[:, 0:1]) * both[:, 1:2] * gain[...].astype(F32)).astype(BF)
    for v in range(N):
        out[v] = normed


def project_kernel(got, weight, query, out):
    for c in range(3):
        acc = None
        for v in range(N):
            term = jnp.dot(
                got[v], weight[c, COLS * v : COLS * v + COLS], preferred_element_type=F32
            )
            acc = term if acc is None else acc + term
        acc = acc.astype(BF)
        if c == 0:
            query[...] = acc
        else:
            for k in range(Z):
                out[k, TOK * (c - 1) : TOK * c] = acc


def attend_kernel(query, own, other, out, scores):
    q = query[...]
    blocks = [(ref, k) for ref in (own, other) for k in range(Z)]
    peak = None
    for i, (ref, k) in enumerate(blocks):
        s = (
            lax.dot_general(
                q, ref[k, 0:TOK], (((1,), (1,)), ((), ())), preferred_element_type=F32
            )
            * SCALE
        )
        scores[:, TOK * i : TOK * i + TOK] = s
        peak = s if peak is None else jnp.maximum(peak, s)
    peak = jnp.max(peak, axis=1, keepdims=True)
    total, acc = None, None
    for i, (ref, k) in enumerate(blocks):
        e = jnp.exp(scores[:, TOK * i : TOK * i + TOK] - peak)
        total = e if total is None else total + e
        term = jnp.dot(e.astype(BF), ref[k, TOK : 2 * TOK], preferred_element_type=F32)
        acc = term if acc is None else acc + term
    context = (acc / jnp.sum(total, axis=1, keepdims=True)).astype(BF)
    for v in range(N):
        out[v] = context


def output_kernel(got, weight, out):
    pairs = [jnp.concatenate([got[h], got[h + 1]], 1) for h in range(0, N, 2)]
    halves = columns_of(pairs, weight)
    for i in range(2):
        out[:, 128 * i : 128 * i + 128] = halves[i].astype(BF)


def shape(dims, kind):
    return jax.ShapeDtypeStruct(dims, kind)


RINGS = [list(range(Z)), list(range(Z, N))]
CORES = [list(range(0, N, 2)), list(range(1, N, 2))]


def exchange(x, axis, groups=None):
    return lax.all_to_all(x, axis, 0, 0, tiled=True, axis_index_groups=groups)


def swap(x, axis, bits):
    return lax.ppermute(x, axis, [(i, i ^ bits) for i in range(N)])


def shards(
    patches,
    slot_variable,
    embed_weight,
    variable_embed,
    norm_gain,
    pool_keys,
    pool_value,
    pool_out,
    block_gain,
    attend_weight,
    out_proj,
):
    v_idx, k_idx = lax.axis_index("var"), lax.axis_index("tok")
    place = jnp.stack([k_idx // 2, k_idx % 2]).astype(jnp.int32)

    rows_of_k = pl.BlockSpec((16, D), lambda i, place: (place[0], 0))
    parts = pl.pallas_call(
        weights_kernel,
        out_shape=shape((N, W_ROWS, 128), BF),
        grid_spec=pltpu.PrefetchScalarGridSpec(
            num_scalar_prefetch=1,
            grid=(1,),
            in_specs=[pl.BlockSpec((COLS, E), lambda i, place: (0, 0)), rows_of_k, rows_of_k],
            out_specs=pl.BlockSpec((N, W_ROWS, 128), lambda i, place: (0, 0, 0)),
        ),
        cost_estimate=pl.CostEstimate(flops=0, bytes_accessed=800_000, transcendentals=0),
    )(place, pool_value, pool_out, out_proj)
    parts = exchange(parts, "var")
    packed = call(
        embed_kernel,
        shape((N, ROWS, 128), BF),
        7,
        (pltpu.VMEM((TOK, 128), F32), pltpu.VMEM((2, R_ST - R_P, TOK), BF)),
        smem=(0, 1),
        flops=2 * SLOTS * TOK * D * 48,
        size=6_000_000,
    )(
        slot_variable,
        place,
        patches,
        embed_weight,
        variable_embed,
        norm_gain[None],
        pool_keys.T,
    )
    parts = call(hand_on_kernel, shape((N * W_ROWS, 128), BF), 2, hbm=(1,), size=600_000)(
        parts, packed
    )
    parts = lax.all_gather(parts, "tok", axis=0)
    got = exchange(packed, "var")
    swapped = swap(got[:, R_U:R_P], "tok", 1)
    gain = lax.dynamic_index_in_dim(norm_gain.reshape(N, Z, 32), v_idx % Z, 1, keepdims=False)

    summed = call(
        pool_kernel,
        shape((4, N * SUM_STEP, 128), F32),
        4,
        (
            pltpu.VMEM((PAIRS * N, TOK), F32),
            pltpu.VMEM((2, PART * LEFT_STEP, TOK), F32),
            pltpu.VMEM((4, PART * ROW_STEP, 128), F32),
        ),
        smem=(0,),
        vmem=26,
        flops=2 * 400_000_000,
        size=5_000_000,
    )(place, got, swapped, gain.reshape(1, WIDE))
    partial, pool_part, proj_part = call(
        values_kernel,
        (
            shape((Z, TOK, E), F32),
            shape((N, 16 * N, 128), BF),
            shape((N, 16 * N, 128), BF),
        ),
        2,
        (pltpu.VMEM((N, 32 * N, E), BF), pltpu.SemaphoreType.DMA((3,))),
        hbm=(1,),
        flops=4 * PART * WIDE * 2048,
        size=9_000_000,
    )(summed, parts)
    pooled = call(pooled_kernel, shape((N, TOK, E), BF), 1, size=1_000_000)(
        exchange(partial, "var", RINGS)
    )
    state, aggregated, stats = call(
        state_kernel,
        (shape((TOK, COLS), F32), shape((TOK, COLS), BF), shape((N, 8, 128), F32)),
        2,
        (pltpu.VMEM((TOK, 128), F32),),
        flops=2 * TOK * 2048 * COLS,
        size=2_000_000,
    )(exchange(pooled, "var"), pool_part)
    gain = lax.dynamic_slice(block_gain, (COLS * v_idx,), (COLS,))[None]
    normed = call(norm_kernel, shape((N, TOK, COLS), BF), 3, size=1_200_000)(
        exchange(stats, "var"), state, gain
    )
    query, kv = call(
        project_kernel,
        (shape((TOK, E), BF), shape((Z, 2 * TOK, E), BF)),
        2,
        flops=2 * TOK * D * 384,
        size=5_000_000,
    )(exchange(normed, "var"), attend_weight)
    kv = exchange(kv, "tok", CORES)
    context = call(
        attend_kernel,
        shape((N, TOK, E), BF),
        3,
        (pltpu.VMEM((TOK, N * TOK), F32),),
        flops=4 * TOK * 2048 * E,
        size=1_500_000,
    )(query, kv, swap(kv, "tok", 1))
    attended = call(
        output_kernel, shape((TOK, COLS), BF), 2, flops=2 * TOK * 2048 * COLS, size=2_000_000
    )(exchange(context, "var"), proj_part)
    return (aggregated, attended)


def solution(mesh):
    return jax.shard_map(
        shards,
        mesh=mesh,
        in_specs=(
            P("var", None, "tok"),
            P("var"),
            P("var", None, None),
            P(),
            P(),
            P(),
            P("tok", "var"),
            P("var", None),
            P(),
            P(None, None, "var"),
            P("var", None),
        ),
        out_specs=(P("tok", "var"), P("tok", "var")),
        check_vma=False,
    )
```

```python
import functools
import math

import jax
import jax.numpy as jnp
from jax import lax
from jax.experimental import pallas as pl
from jax.experimental.pallas import tpu as pltpu
from jax.sharding import PartitionSpec as P

F32 = jnp.float32
BF = jnp.bfloat16
N = 16
SLOTS = 6
TOK = 128
COLS = 256
D = 4096
E = 128
SCALE = 1.0 / math.sqrt(128)

Z = 8
WIDE = 512
PART = 64
PAIRS = 48
ROW_STEP, LEFT_STEP, SUM_STEP = 100, 36, 65


R_U, R_P, R_WH, R_WL, R_M, R_ST, ROWS = 0, 192, 240, 288, 336, 368, 416
W_V, W_P, W_O, W_ROWS = 0, 32, 48, 64


def split2(x):
    hi = x.astype(BF)
    return hi, (x - hi.astype(F32)).astype(BF)


def split3(x):
    hi = x.astype(BF)
    rest = x - hi.astype(F32)
    mid = rest.astype(BF)
    return hi, mid, (rest - mid.astype(F32)).astype(BF)


def call(kernel, out_shape, n_in, scratch=(), smem=(), hbm=(), vmem=16, flops=0, size=0):
    spaces = {i: pltpu.SMEM for i in smem} | {i: pltpu.HBM for i in hbm}
    vm = pl.BlockSpec(memory_space=pltpu.VMEM)
    many = isinstance(out_shape, (tuple, list))
    return pl.pallas_call(
        kernel,
        out_shape=out_shape,
        in_specs=[pl.BlockSpec(memory_space=spaces.get(i, pltpu.VMEM)) for i in range(n_in)],
        out_specs=[vm] * len(out_shape) if many else vm,
        scratch_shapes=list(scratch),
        compiler_params=pltpu.CompilerParams(vmem_limit_bytes=vmem * 1024 * 1024),
        cost_estimate=pl.CostEstimate(flops=flops, bytes_accessed=size, transcendentals=0),
    )


def weights_kernel(place, value, pool_rows, proj_rows, out):
    half = place[1]
    for v in range(N):
        z = v % Z
        out[v, W_V : W_V + 32] = value[32 * z : 32 * z + 32]
        at = pl.ds(pl.multiple_of(COLS * v + 128 * half, 128), 128)
        out[v, W_P : W_P + 16] = pool_rows[:, at]
        out[v, W_O : W_O + 16] = proj_rows[:, at]


def chunks(x, z, j):
    at = [256 * k + 32 * z for k in range(4 * j, 4 * j + 4)]
    return jnp.concatenate([x[:, a : a + 32] for a in at], 1)


def embed_kernel(slot, place, patches, weight, table, gain, keys, out, columns, common):
    wide = table.shape[0]
    row = lax.broadcasted_iota(jnp.int32, (8, wide), 0)
    col = lax.broadcasted_iota(jnp.int32, (8, wide), 1)
    pick = jnp.zeros((8, wide), F32)
    for s in range(SLOTS):
        pick = jnp.where((row == s) & (col == slot[s]), 1.0, pick)
    var_rows = jnp.dot(pick.astype(BF), table[...], preferred_element_type=F32)
    gain_row = gain[...].astype(F32)
    columns[...] = jnp.zeros_like(columns)
    scores = []
    for s in range(SLOTS):
        emb = lax.dot_general(
            patches[s], weight[s], (((0,), (0,)), ((), ())), preferred_element_type=F32
        )
        emb = emb + var_rows[s : s + 1]
        mean = jnp.sum(emb, axis=1, keepdims=True) * (1.0 / D)
        emb = emb - mean
        spread = jnp.sum(emb * emb, axis=1, keepdims=True) * (1.0 / D)
        rstd = lax.rsqrt(spread + 1e-05)
        normed = (emb * rstd * gain_row).astype(BF)
        score = lax.dot_general(
            keys[...], normed, (((1,), (1,)), ((), ())), preferred_element_type=F32
        )
        scores.append(jnp.where(slot[s] >= 0, score * SCALE, -1e30))
        columns[:, s : s + 1] = mean
        columns[:, 6 + s : 7 + s] = rstd
    turned = jnp.transpose(columns[...])
    top = scores[0]
    for s in range(1, SLOTS):
        top = jnp.maximum(top, scores[s])
    weights = [jnp.where(slot[s] >= 0, jnp.exp(scores[s] - top), 0.0) for s in range(SLOTS)]

    def beside(low, high, x):
        at = slice(PART * x, PART * x + PART)
        return jnp.concatenate([low[:, at], high[:, at]], 1)

    tops = [t.astype(F32) for t in split3(top)] + [jnp.zeros((N, TOK), F32)]
    for x in range(2):
        for i in range(3):
            a = 16 * i
            low, high = patches[i].astype(F32), patches[i + 3].astype(F32)
            common[x, a : a + 16] = beside(low, high, x).astype(BF)
            hi, lo = split2(beside(weights[i], weights[i + 3], x))
            common[x, R_WH - R_P + a : R_WH - R_P + a + 16] = hi
            common[x, R_WL - R_P + a : R_WL - R_P + a + 16] = lo
        for i in range(2):
            a = R_M - R_P + 16 * i
            common[x, a : a + 16] = beside(tops[2 * i], tops[2 * i + 1], x).astype(BF)
        stats = []
        for first in (0, 6):
            both = beside(turned[first : first + 3], turned[first + 3 : first + 6], x)
            stats.extend(part.astype(F32) for part in split3(both))
        for z in range(Z):
            out[Z * x + z, R_P:R_ST] = common[x]
            rows = stats + [chunks(var_rows, z, j)[:6] for j in range(4)]
            rows.append(jnp.zeros((6, TOK), F32))
            out[Z * x + z, R_ST:] = jnp.concatenate(rows, 0).astype(BF)
    for i in range(3):
        wide = weight[3 * place[1] + i].astype(F32)
        for z in range(Z):
            for j in range(4):
                a = R_U + 48 * j + 16 * i
                part = chunks(wide, z, j).astype(BF)
                for x in range(2):
                    out[Z * x + z, a : a + 16] = part


def hand_on_kernel(parts, early, out):
    for first, last in ((W_V, W_P), (W_P, W_O), (W_O, W_ROWS)):
        size = last - first
        for h in range(N):
            a = N * first + size * h
            out[a : a + size] = parts[h, first:last]


def pool_kernel(place, got, swapped, gain, high_out, low_out, weights, turned, rows, summed):
    tops = []
    for v in range(N):
        m = [got[v, R_M + 16 * i : R_M + 16 * i + 16].astype(F32) for i in range(2)]
        tops.append((m[0][:, :PART] + m[0][:, PART:]) + m[1][:, :PART])
    top = tops[0]
    for v in range(1, N):
        top = jnp.maximum(top, tops[v])
    total = jnp.zeros((N, TOK), F32)
    for v in range(N):
        factor = jnp.exp(tops[v] - top)
        factor = jnp.concatenate([factor, factor], 1)
        for i in range(3):
            a = 16 * i
            w = got[v, R_WH + a : R_WH + a + 16].astype(F32) + got[
                v, R_WL + a : R_WL + a + 16
            ].astype(F32)
            w = w * factor
            total = total + w
            weights[48 * v + a : 48 * v + a + 16] = w
    inverse = 1.0 / (total[:, :PART] + total[:, PART:])
    inverse = jnp.concatenate([inverse, inverse], 1)
    odd = lax.broadcasted_iota(jnp.int32, (PAIRS, TOK), 1) % 2 == 1
    for h in range(0, N, 2):
        w = [weights[pl.ds(h + n, PAIRS, stride=16)] * inverse[h + n : h + n + 1] for n in range(2)]
        low = jnp.concatenate([x[:, :PART] for x in w], 1)
        high = jnp.concatenate([x[:, PART:] for x in w], 1)
        gap = jnp.zeros((ROW_STEP - 2 * PAIRS, TOK), F32)
        parts = [jnp.where(odd, 0.0, low), jnp.where(odd, 0.0, high), gap]
        parts += [jnp.where(odd, low, 0.0), jnp.where(odd, high, 0.0)]
        parts.append(jnp.zeros((256 - ROW_STEP - 2 * PAIRS, TOK), F32))
        w = jnp.concatenate(parts, 0)
        for j in range(2):
            part = jnp.transpose(w[128 * j : 128 * j + 128])
            hi = part.astype(BF).astype(F32)
            lo = (part - hi).astype(BF).astype(F32)
            for n in range(2):
                at = slice(PART * n, PART * n + PART)
                turned[j, pl.ds(h + n, PART, stride=LEFT_STEP)] = hi[at]
                turned[j, pl.ds(16 + h + n, PART, stride=LEFT_STEP)] = lo[at]
    gain_row = gain[...].astype(F32)
    even_core = place[1] == 0

    def source(v, carry):
        st = got[v, R_ST:ROWS].astype(F32)
        mean = (st[0:3] + st[3:6]) + st[6:9]
        rstd = (st[9:12] + st[12:15]) + st[15:18]
        both = jnp.transpose(jnp.concatenate([mean, rstd, jnp.zeros((122, TOK), F32)], 0))
        for i in range(3):
            p = got[v, R_P + 16 * i : R_P + 16 * i + 16]
            us = []
            for ref in (got, swapped):
                at = [48 * j + 16 * i for j in range(4)]
                us.append(jnp.concatenate([ref[v, a : a + 16] for a in at], 1))
            sides = (jnp.where(even_core, us[0], us[1]), jnp.where(even_core, us[1], us[0]))
            for n in range(2):
                at = slice(PART * n, PART * n + PART)
                emb = lax.dot_general(
                    p[:, at], sides[n], (((0,), (0,)), ((), ())), preferred_element_type=F32
                )
                col_mean, col_rstd = both[at, i : i + 1], both[at, 3 + i : 4 + i]
                for j in range(4):
                    a = 18 + 6 * j + 3 * n + i
                    x = emb[:, 128 * j : 128 * j + 128] + st[a : a + 1]
                    x = (x - col_mean) * col_rstd * gain_row[:, 128 * j : 128 * j + 128]
                    rows[j, pl.ds(PAIRS * n + 3 * v + i, PART, stride=ROW_STEP)] = x
        return carry

    for j in range(4):
        for i in range(2 * PAIRS, ROW_STEP):
            rows[j, pl.ds(i, PART, stride=ROW_STEP)] = jnp.zeros((PART, 128), F32)
    lax.fori_loop(0, N, source, 0, unroll=4)

    for j in range(2):
        for i in range(32, LEFT_STEP):
            turned[j, pl.ds(i, PART, stride=LEFT_STEP)] = jnp.zeros((PART, 128), F32)

    def two_tokens(g, carry):
        at = pl.ds(pl.multiple_of(g * 2 * LEFT_STEP, 8), 2 * LEFT_STEP)
        lhs = jnp.concatenate([turned[0, at], turned[1, at][:, : 2 * ROW_STEP - 128]], 1)
        span = pl.ds(pl.multiple_of(g * 2 * ROW_STEP, 8), 2 * ROW_STEP)
        rhs = jnp.concatenate([rows[j, span] for j in range(4)], 1)
        y = jnp.dot(lhs.astype(BF), rhs.astype(BF), preferred_element_type=F32)
        for q in range(2):
            a = LEFT_STEP * q
            part = y[a : a + 16] + y[a + 16 : a + 32]
            for j in range(4):
                summed[j, pl.ds(2 * g + q, 16, stride=SUM_STEP)] = part[
                    :, 128 * j : 128 * j + 128
                ]
        return carry

    lax.fori_loop(0, PART // 2, two_tokens, 0, unroll=4)
    for h in range(N):
        at = slice(SUM_STEP * h, SUM_STEP * h + PART)
        hi, lo = split2(jnp.concatenate([summed[j, at] for j in range(4)], 1))
        high_out[PART * h : PART * h + PART] = hi
        low_out[PART * h : PART * h + PART] = lo


def values_kernel(high, low, parts, out, pool_part, proj_part, value, sems):
    copies = []
    for i, (row, into) in enumerate(((W_V, value), (W_P, pool_part), (W_O, proj_part))):
        span = pl.ds(N * row, into.shape[1])
        copies.append(pltpu.make_async_copy(parts.at[:, span], into, sems.at[i]))
    for copy in copies:
        copy.start()
    copies[0].wait()
    for h in range(N):
        at = slice(PART * h, PART * h + PART)
        right = jnp.concatenate([value[k, 32 * h : 32 * h + 32] for k in range(N)], 0)
        whole = jnp.dot(jnp.concatenate([high[at], low[at]], 0), right, preferred_element_type=F32)
        out[h // 2, PART * (h % 2) : PART * (h % 2) + PART] = whole[:PART] + whole[PART:]
    for copy in copies[1:]:
        copy.wait()


def pooled_kernel(got, out):
    total = got[0]
    for z in range(1, Z):
        total = total + got[z]
    total = total.astype(BF)
    for v in range(N):
        out[v] = total


def columns_of(pairs, weight):
    halves = []
    for half in range(2):
        acc = None
        for i, left in enumerate(pairs):
            right = jnp.concatenate(
                [
                    weight[2 * j + half, a : a + 16]
                    for a in (32 * i, 32 * i + 16)
                    for j in range(8)
                ],
                0,
            )
            term = jnp.dot(left, right, preferred_element_type=F32)
            acc = term if acc is None else acc + term
        halves.append(acc)
    return halves


def state_kernel(got, weight, state, aggregated, stats, columns):
    pairs = []
    for z in range(Z):
        sides = [
            jnp.concatenate([got[v, 0:PART], got[v, PART : 2 * PART]], 1) for v in (z, Z + z)
        ]
        pairs.append(jnp.concatenate(sides, 0))
    halves = columns_of(pairs, weight)
    mean = jnp.sum(halves[0] + halves[1], axis=1, keepdims=True) * (1.0 / COLS)
    spread = jnp.zeros((TOK, 128), F32)
    for i in range(2):
        state[:, 128 * i : 128 * i + 128] = halves[i]
        aggregated[:, 128 * i : 128 * i + 128] = halves[i].astype(BF)
        gap = halves[i] - mean
        spread = spread + gap * gap
    columns[...] = jnp.zeros_like(columns)
    columns[:, 0:1] = mean
    columns[:, 1:2] = jnp.sum(spread, axis=1, keepdims=True)
    turned = jnp.transpose(columns[...])[0:8]
    for v in range(N):
        stats[v] = turned


def norm_kernel(got, state, gain, out):
    mean = got[0, 0:1]
    for v in range(1, N):
        mean = mean + got[v, 0:1]
    mean = mean * (1.0 / N)
    spread = jnp.zeros((1, TOK), F32)
    for v in range(N):
        gap = got[v, 0:1] - mean
        spread = spread + (got[v, 1:2] + COLS * gap * gap)
    rstd = lax.rsqrt(spread * (1.0 / D) + 1e-05)
    both = jnp.transpose(jnp.concatenate([mean, rstd, jnp.zeros((126, TOK), F32)], 0))
    normed = ((state[...] - both[:, 0:1]) * both[:, 1:2] * gain[...].astype(F32)).astype(BF)
    for v in range(N):
        out[v] = normed


def project_kernel(got, weight, query, out):
    for c in range(3):
        acc = None
        for v in range(N):
            term = jnp.dot(
                got[v], weight[c, COLS * v : COLS * v + COLS], preferred_element_type=F32
            )
            acc = term if acc is None else acc + term
        acc = acc.astype(BF)
        if c == 0:
            query[...] = acc
        else:
            for k in range(Z):
                out[k, TOK * (c - 1) : TOK * c] = acc


def attend_kernel(query, own, other, out, scores):
    q = query[...]
    blocks = [(ref, k) for ref in (own, other) for k in range(Z)]
    peak = None
    for i, (ref, k) in enumerate(blocks):
        s = (
            lax.dot_general(
                q, ref[k, 0:TOK], (((1,), (1,)), ((), ())), preferred_element_type=F32
            )
            * SCALE
        )
        scores[:, TOK * i : TOK * i + TOK] = s
        peak = s if peak is None else jnp.maximum(peak, s)
    peak = jnp.max(peak, axis=1, keepdims=True)
    total, acc = None, None
    for i, (ref, k) in enumerate(blocks):
        e = jnp.exp(scores[:, TOK * i : TOK * i + TOK] - peak)
        total = e if total is None else total + e
        term = jnp.dot(e.astype(BF), ref[k, TOK : 2 * TOK], preferred_element_type=F32)
        acc = term if acc is None else acc + term
    context = (acc / jnp.sum(total, axis=1, keepdims=True)).astype(BF)
    for v in range(N):
        out[v] = context


def output_kernel(got, weight, out):
    pairs = [jnp.concatenate([got[h], got[h + 1]], 1) for h in range(0, N, 2)]
    halves = columns_of(pairs, weight)
    for i in range(2):
        out[:, 128 * i : 128 * i + 128] = halves[i].astype(BF)


def shape(dims, kind):
    return jax.ShapeDtypeStruct(dims, kind)


RINGS = [list(range(Z)), list(range(Z, N))]
CORES = [list(range(0, N, 2)), list(range(1, N, 2))]


def exchange(x, axis, groups=None):
    return lax.all_to_all(x, axis, 0, 0, tiled=True, axis_index_groups=groups)


def swap(x, axis, bits):
    return lax.ppermute(x, axis, [(i, i ^ bits) for i in range(N)])


def shards(
    patches,
    slot_variable,
    embed_weight,
    variable_embed,
    norm_gain,
    pool_keys,
    pool_value,
    pool_out,
    block_gain,
    attend_weight,
    out_proj,
):
    v_idx, k_idx = lax.axis_index("var"), lax.axis_index("tok")
    place = jnp.stack([k_idx // 2, k_idx % 2]).astype(jnp.int32)

    rows_of_k = pl.BlockSpec((16, D), lambda i, place: (place[0], 0))
    parts = pl.pallas_call(
        weights_kernel,
        out_shape=shape((N, W_ROWS, 128), BF),
        grid_spec=pltpu.PrefetchScalarGridSpec(
            num_scalar_prefetch=1,
            grid=(1,),
            in_specs=[pl.BlockSpec((COLS, E), lambda i, place: (0, 0)), rows_of_k, rows_of_k],
            out_specs=pl.BlockSpec((N, W_ROWS, 128), lambda i, place: (0, 0, 0)),
        ),
        cost_estimate=pl.CostEstimate(flops=0, bytes_accessed=800_000, transcendentals=0),
    )(place, pool_value, pool_out, out_proj)
    parts = exchange(parts, "var")
    packed = call(
        embed_kernel,
        shape((N, ROWS, 128), BF),
        7,
        (pltpu.VMEM((TOK, 128), F32), pltpu.VMEM((2, R_ST - R_P, TOK), BF)),
        smem=(0, 1),
        flops=2 * SLOTS * TOK * D * 48,
        size=6_000_000,
    )(
        slot_variable,
        place,
        patches,
        embed_weight,
        variable_embed,
        norm_gain[None],
        pool_keys.T,
    )
    parts = call(hand_on_kernel, shape((N * W_ROWS, 128), BF), 2, hbm=(1,), size=600_000)(
        parts, packed
    )
    parts = lax.all_gather(parts, "tok", axis=0)
    got = exchange(packed, "var")
    swapped = swap(got[:, R_U:R_P], "tok", 1)
    gain = lax.dynamic_index_in_dim(norm_gain.reshape(N, Z, 32), v_idx % Z, 1, keepdims=False)

    high, low = call(
        pool_kernel,
        (shape((N * PART, WIDE), BF), shape((N * PART, WIDE), BF)),
        4,
        (
            pltpu.VMEM((PAIRS * N, TOK), F32),
            pltpu.VMEM((2, PART * LEFT_STEP, TOK), F32),
            pltpu.VMEM((4, PART * ROW_STEP, 128), F32),
            pltpu.VMEM((4, N * SUM_STEP, 128), F32),
        ),
        smem=(0,),
        vmem=26,
        flops=2 * 400_000_000,
        size=5_000_000,
    )(place, got, swapped, gain.reshape(1, WIDE))
    partial, pool_part, proj_part = call(
        values_kernel,
        (
            shape((Z, TOK, E), F32),
            shape((N, 16 * N, 128), BF),
            shape((N, 16 * N, 128), BF),
        ),
        3,
        (pltpu.VMEM((N, 32 * N, E), BF), pltpu.SemaphoreType.DMA((3,))),
        hbm=(2,),
        flops=4 * PART * WIDE * 2048,
        size=9_000_000,
    )(high, low, parts)
    pooled = call(pooled_kernel, shape((N, TOK, E), BF), 1, size=1_000_000)(
        exchange(partial, "var", RINGS)
    )
    state, aggregated, stats = call(
        state_kernel,
        (shape((TOK, COLS), F32), shape((TOK, COLS), BF), shape((N, 8, 128), F32)),
        2,
        (pltpu.VMEM((TOK, 128), F32),),
        flops=2 * TOK * 2048 * COLS,
        size=2_000_000,
    )(exchange(pooled, "var"), pool_part)
    gain = lax.dynamic_slice(block_gain, (COLS * v_idx,), (COLS,))[None]
    normed = call(norm_kernel, shape((N, TOK, COLS), BF), 3, size=1_200_000)(
        exchange(stats, "var"), state, gain
    )
    query, kv = call(
        project_kernel,
        (shape((TOK, E), BF), shape((Z, 2 * TOK, E), BF)),
        2,
        flops=2 * TOK * D * 384,
        size=5_000_000,
    )(exchange(normed, "var"), attend_weight)
    kv = exchange(kv, "tok", CORES)
    context = call(
        attend_kernel,
        shape((N, TOK, E), BF),
        3,
        (pltpu.VMEM((TOK, N * TOK), F32),),
        flops=4 * TOK * 2048 * E,
        size=1_500_000,
    )(query, kv, swap(kv, "tok", 1))
    attended = call(
        output_kernel, shape((TOK, COLS), BF), 2, flops=2 * TOK * 2048 * COLS, size=2_000_000
    )(exchange(context, "var"), proj_part)
    return (aggregated, attended)


def solution(mesh):
    return jax.shard_map(
        shards,
        mesh=mesh,
        in_specs=(
            P("var", None, "tok"),
            P("var"),
            P("var", None, None),
            P(),
            P(),
            P(),
            P("tok", "var"),
            P("var", None),
            P(),
            P(None, None, "var"),
            P("var", None),
        ),
        out_specs=(P("tok", "var"), P("tok", "var")),
        check_vma=False,
    )
```
